32 devices in a mesh: ctx: 16 (over z, y, x), heads: 2 (over core).
Axes of the slice: x: 2, y: 2, z: 4, core: 2. Of those that a mesh axis runs over, the one named last changes fastest.
Arguments:
- resid_in: bfloat16 [2048, 5376], P('ctx', 'heads'), may hold values from -6 to 6
- first_layer_queries: bfloat16 [2048, 4096], P('ctx', 'heads'), may hold values from -270 to 270
- first_layer_keys: bfloat16 [2048, 2048], P('ctx', 'heads'), may hold values from -7 to 7
- first_layer_values: bfloat16 [2048, 2048], P('ctx', 'heads'), may hold values from -6 to 6
- out_one: bfloat16 [4096, 5376], P('heads'), may hold values from -6 to 6
- post_gain: float32 [5376], replicated, may hold values from 0.1 to 1.9
- pre_gain: float32 [5376], replicated, may hold values from 0.1 to 1.9
- proj_query: bfloat16 [5376, 4096], P('ctx', 'heads'), may hold values from -30 to 30
- key_projection: bfloat16 [5376, 2048], P('ctx', 'heads'), may hold values from -1 to 1
- value_projection: bfloat16 [5376, 2048], P('ctx', 'heads'), may hold values from -0.078125 to 0.078125
- window: int32 [32], P('heads'), may hold values from 512 to 1024, as said below
- positions: int32 [2048], replicated, may hold values from 0 to 1023, as said below
Outputs:
- resid_out: bfloat16 [2048, 5376], P('ctx', 'heads')
- attended: bfloat16 [2048, 4096], P('ctx', 'heads')
The draws below stay inside these ranges and needn't reach their ends.
Inputs may be any that keep to these rules, and one draw needn't show every extreme that they name: Each query head's window counts back from and includes its own token; some head's window is exactly 1024. `positions`: tokens form three packed documents: a position is 0 at a document's first token and one more than the previous token's otherwise; one document has exactly 1024 tokens and none has more.
All inputs are finite; a program needn't handle non-finite values.
Results may differ from the reference program's by a relative error of at most 0.03.
Values may be sent and summed in bfloat16 or wider, within the bound.
A program may use at most 128 MiB of HBM per device.

```python
import math
import jax
import jax.numpy as jnp
from jax import lax

MODEL_WIDTH = 5376
QUERY_HEAD_COUNT = 32
KEY_VALUE_HEADS = 16
HEAD_SIZE = 128
LONGEST_WINDOW = 1024
TOK_DEV = 128
SEQUENCE_TOKENS = 2048
N_CTX = 16
N_HEADS = 2


def clipped_normal(key, shape):
    return jax.random.truncated_normal(key, -6.0, 6.0, shape, jnp.float32)


def first_keys_full(key):
    base_value = clipped_normal(jax.random.fold_in(key, 101), (SEQUENCE_TOKENS, KEY_VALUE_HEADS * HEAD_SIZE))
    return base_value


def second_keys_full(key):
    return clipped_normal(jax.random.fold_in(key, 201), (MODEL_WIDTH, KEY_VALUE_HEADS * HEAD_SIZE)) / jnp.sqrt(jnp.float32(MODEL_WIDTH))


def draw_first_layer_keys(key, part):
    return first_keys_full(key).astype(jnp.bfloat16)


def draw_first_layer_queries(key, part):
    drawn = clipped_normal(jax.random.fold_in(key, 103), (SEQUENCE_TOKENS, QUERY_HEAD_COUNT * HEAD_SIZE))
    return drawn.astype(jnp.bfloat16)


def draw_out_one(key, part):
    drawn = clipped_normal(jax.random.fold_in(key, 105), (QUERY_HEAD_COUNT * HEAD_SIZE, MODEL_WIDTH)) / jnp.sqrt(jnp.float32(QUERY_HEAD_COUNT * HEAD_SIZE))
    column = jnp.arange(MODEL_WIDTH, dtype=jnp.float32) / MODEL_WIDTH
    ramp = jnp.power(3.0, column)
    return (drawn * ramp[None, :]).astype(jnp.bfloat16)


def draw_key_projection(key, part):
    return second_keys_full(key).astype(jnp.bfloat16)


def draw_proj_query(key, part):
    drawn = clipped_normal(jax.random.fold_in(key, 202), (MODEL_WIDTH, QUERY_HEAD_COUNT * HEAD_SIZE)) / jnp.sqrt(jnp.float32(MODEL_WIDTH))
    return drawn.astype(jnp.bfloat16)


def draw_window(key, part):
    widths = jax.random.randint(jax.random.fold_in(key, 301), (QUERY_HEAD_COUNT,), LONGEST_WINDOW // 2, LONGEST_WINDOW + 1)
    chosen = jax.random.randint(jax.random.fold_in(key, 302), (), 0, QUERY_HEAD_COUNT)
    return jnp.where(jnp.arange(QUERY_HEAD_COUNT) == chosen, LONGEST_WINDOW, widths).astype(jnp.int32)


def draw_positions(key, part):
    half_seq = SEQUENCE_TOKENS // 2
    first_cut = jax.random.randint(jax.random.fold_in(key, 401), (), 1, half_seq).astype(jnp.int32)
    cuts = jnp.stack([first_cut, first_cut + half_seq])
    row_ids = jnp.arange(SEQUENCE_TOKENS, dtype=jnp.int32)
    starts = jnp.max(jnp.where(cuts[None, :] <= row_ids[:, None], cuts[None, :], 0), axis=1)
    return (row_ids - starts).astype(jnp.int32)


def block_levels(own_key, extent, shards, least, high):
    def one(dim, blocks):
        draws = jax.random.uniform(jax.random.fold_in(jax.random.fold_in(own_key, 6), dim), (blocks,), jnp.float32, least / len(shards), high / len(shards))
        return jnp.repeat(jnp.exp(draws), extent[dim] // blocks).reshape((-1,) + (1,) * (len(extent) - dim - 1))

    factor_of = one(*shards[0])
    for cut in shards[1:]:
        factor_of = factor_of * one(*cut)
    return factor_of


def noise(rng, extent, scale, reach, shards=(), held_as=jnp.bfloat16):
    values = jax.random.normal(rng, extent, jnp.float32) * scale
    if len(shards) > 0:
        values = block_levels(rng, extent, shards, -0.22, 0.18) * values
    return jnp.clip(values, min=-reach, max=reach).astype(held_as)


def setup_inputs(seed: int = 0) -> dict:
    key_of = jax.random.split(jax.random.key(seed), 13)
    return {
        "resid_in": noise(key_of[0], (SEQUENCE_TOKENS, MODEL_WIDTH), 1.0, 6.0, ((0, 16), (1, 2))),
        "first_layer_queries": draw_first_layer_queries(jax.random.fold_in(key_of[12], 71), 0),
        "first_layer_keys": draw_first_layer_keys(jax.random.fold_in(key_of[12], 71), 0),
        "first_layer_values": noise(key_of[3], (SEQUENCE_TOKENS, KEY_VALUE_HEADS * HEAD_SIZE), 1.0, 6.0, ((0, 16), (1, 2))),
        "out_one": draw_out_one(jax.random.fold_in(key_of[12], 71), 0),
        "post_gain": jnp.clip(1.0 + 0.18 * jax.random.normal(key_of[5], (MODEL_WIDTH,), jnp.float32), 0.1, 1.9),
        "pre_gain": jnp.clip(1.0 + 0.18 * jax.random.normal(key_of[6], (MODEL_WIDTH,), jnp.float32), 0.1, 1.9),
        "proj_query": draw_proj_query(jax.random.fold_in(key_of[12], 71), 0),
        "key_projection": draw_key_projection(jax.random.fold_in(key_of[12], 71), 0),
        "value_projection": noise(key_of[9], (MODEL_WIDTH, KEY_VALUE_HEADS * HEAD_SIZE), MODEL_WIDTH ** -0.5, 0.078125, ((0, 16), (1, 2))),
        "window": draw_window(jax.random.fold_in(key_of[12], 71), 0),
        "positions": draw_positions(jax.random.fold_in(key_of[12], 71), 0),
    }


SCALE = 168.0 ** (-0.5)
EPS = 1e-06
THETA = 1000000.0
POSITION_FACTOR = 0.125

def apply_rotary(values, pos_rows, factor):
    half_dim = values.shape[-1] // 2
    speeds = THETA ** (-(jnp.arange(half_dim, dtype=jnp.float32) * 2.0 / values.shape[-1]))
    angles = (pos_rows.astype(jnp.float32) * factor)[:, None] * speeds[None, :]
    cosine = jnp.cos(angles)[:, None, :]
    sine_part = jnp.sin(angles)[:, None, :]
    front_half = values[..., :half_dim]
    back_half = values[..., half_dim:]
    return jnp.concatenate([front_half * cosine - back_half * sine_part, back_half * cosine + front_half * sine_part], axis=-1)

def masked_attention(query_row_block, key_row_block, value_row_block, query_tok, key_tok, query_pos, key_pos, window_limits):
    scores = jnp.einsum('qagd,kad->qagk', query_row_block.astype(jnp.float32), key_row_block.astype(jnp.float32)) * SCALE
    distance = query_tok[:, None] - key_tok[None, :]
    base_ok = (distance >= 0) & (key_tok[None, :] >= 0) & (query_pos[:, None] - key_pos[None, :] == distance)
    visible = base_ok[:, None, None, :] & (distance[:, None, None, :] < window_limits[None, :, :, None])
    row_peak = lax.optimization_barrier(jnp.max(jnp.where(visible, scores, -1e+30), axis=-1, keepdims=True))
    lifted = jnp.where(visible, jnp.exp(scores - row_peak), 0.0)
    row_total = lax.optimization_barrier(jnp.sum(lifted, axis=-1))
    weights = lifted.astype(jnp.bfloat16)
    mixed = jnp.einsum('qagk,kad->qagd', weights.astype(jnp.float32), value_row_block.astype(jnp.float32))
    return (mixed / row_total[..., None]).astype(jnp.bfloat16)

def reference(resid_in, first_layer_queries, first_layer_keys, first_layer_values, out_one, post_gain, pre_gain, proj_query, key_projection, value_projection, window, positions):
    token_sequence = resid_in.shape[0]
    group_length = QUERY_HEAD_COUNT // KEY_VALUE_HEADS
    tokens_all = jnp.arange(token_sequence, dtype=jnp.int32)
    rows_per_block = math.gcd(token_sequence, 512)
    padded_keys = jnp.concatenate([jnp.zeros((LONGEST_WINDOW, KEY_VALUE_HEADS * HEAD_SIZE), jnp.bfloat16), first_layer_keys], axis=0)
    padded_values = jnp.concatenate([jnp.zeros((LONGEST_WINDOW, KEY_VALUE_HEADS * HEAD_SIZE), jnp.bfloat16), first_layer_values], axis=0)
    tok_pad = jnp.arange(-LONGEST_WINDOW, token_sequence, dtype=jnp.int32)
    pos_pad = jnp.concatenate([jnp.zeros((LONGEST_WINDOW,), jnp.int32), positions], axis=0)
    window_limits = window.reshape(KEY_VALUE_HEADS, group_length)

    def layer_one_block(start_index):
        query_row_block = lax.dynamic_slice_in_dim(first_layer_queries, start_index, rows_per_block, 0).reshape(rows_per_block, KEY_VALUE_HEADS, group_length, HEAD_SIZE)
        key_row_block = lax.dynamic_slice_in_dim(padded_keys, start_index, rows_per_block + LONGEST_WINDOW, 0).reshape(rows_per_block + LONGEST_WINDOW, KEY_VALUE_HEADS, HEAD_SIZE)
        value_row_block = lax.dynamic_slice_in_dim(padded_values, start_index, rows_per_block + LONGEST_WINDOW, 0).reshape(rows_per_block + LONGEST_WINDOW, KEY_VALUE_HEADS, HEAD_SIZE)
        key_tok = lax.dynamic_slice_in_dim(tok_pad, start_index, rows_per_block + LONGEST_WINDOW, 0)
        key_pos = lax.dynamic_slice_in_dim(pos_pad, start_index, rows_per_block + LONGEST_WINDOW, 0)
        query_tok = start_index + jnp.arange(rows_per_block, dtype=jnp.int32)
        query_pos = lax.dynamic_slice_in_dim(positions, start_index, rows_per_block, 0)
        result = masked_attention(query_row_block, key_row_block, value_row_block, query_tok, key_tok, query_pos, key_pos, window_limits)
        return result.reshape(rows_per_block, QUERY_HEAD_COUNT * HEAD_SIZE)
    block_starts = jnp.arange(0, token_sequence, rows_per_block, dtype=jnp.int32)
    attend_one = lax.map(layer_one_block, block_starts).reshape(token_sequence, QUERY_HEAD_COUNT * HEAD_SIZE)
    group_cols = QUERY_HEAD_COUNT * HEAD_SIZE // N_HEADS

    def add_group(index, combined):
        index = jnp.asarray(index).astype(jnp.int32)
        columns = lax.dynamic_slice_in_dim(attend_one, index * group_cols, group_cols, 1)
        rows_out = lax.dynamic_slice_in_dim(out_one, index * group_cols, group_cols, 0)
        term = jnp.dot(columns, rows_out, preferred_element_type=jnp.float32).astype(jnp.bfloat16)
        term = lax.optimization_barrier(term)
        return combined + term.astype(jnp.float32)
    combined = lax.fori_loop(0, N_HEADS, add_group, jnp.zeros((token_sequence, MODEL_WIDTH), jnp.float32))
    post_scaled = combined * lax.rsqrt(lax.optimization_barrier(jnp.mean(combined * combined, axis=1, keepdims=True)) + EPS)
    resid_out = (resid_in.astype(jnp.float32) + post_gain[None, :] * post_scaled).astype(jnp.bfloat16)
    residual_rows = resid_out.astype(jnp.float32)
    normalized_rows = (pre_gain[None, :] * residual_rows * lax.rsqrt(lax.optimization_barrier(jnp.mean(residual_rows * residual_rows, axis=1, keepdims=True)) + EPS)).astype(jnp.bfloat16)
    second_layer_query = jnp.dot(normalized_rows, proj_query, preferred_element_type=jnp.float32).reshape(token_sequence, QUERY_HEAD_COUNT, HEAD_SIZE)
    second_layer_query = apply_rotary(second_layer_query, positions, POSITION_FACTOR).astype(jnp.bfloat16).reshape(token_sequence, KEY_VALUE_HEADS, group_length, HEAD_SIZE)
    second_layer_key = jnp.dot(normalized_rows, key_projection, preferred_element_type=jnp.float32).reshape(token_sequence, KEY_VALUE_HEADS, HEAD_SIZE)
    second_layer_key = apply_rotary(second_layer_key, positions, POSITION_FACTOR).astype(jnp.bfloat16)
    second_layer_value = jnp.dot(normalized_rows, value_projection, preferred_element_type=jnp.float32).astype(jnp.bfloat16).reshape(token_sequence, KEY_VALUE_HEADS, HEAD_SIZE)
    widened_limits = jnp.full((KEY_VALUE_HEADS, group_length), token_sequence + 1, jnp.int32)
    query_block = math.gcd(token_sequence, 128)

    def layer_two_block(start_index):
        query_row_block = lax.dynamic_slice_in_dim(second_layer_query, start_index, query_block, 0)
        query_tok = start_index + jnp.arange(query_block, dtype=jnp.int32)
        query_pos = lax.dynamic_slice_in_dim(positions, start_index, query_block, 0)
        result = masked_attention(query_row_block, second_layer_key, second_layer_value, query_tok, tokens_all, query_pos, positions, widened_limits)
        return result.reshape(query_block, QUERY_HEAD_COUNT * HEAD_SIZE)
    two_starts = jnp.arange(0, token_sequence, query_block, dtype=jnp.int32)
    attended_tok = lax.map(layer_two_block, two_starts).reshape(token_sequence, QUERY_HEAD_COUNT * HEAD_SIZE)
    half_rows = TOK_DEV // 2
    device_of = tokens_all // TOK_DEV
    local_row = tokens_all % TOK_DEV
    order = jnp.where(local_row < half_rows, 2 * device_of * half_rows + local_row, (2 * N_CTX - 1 - 2 * device_of) * half_rows + local_row - half_rows).astype(jnp.int32)
    attended = jnp.take(attended_tok, order, axis=0)
    return (resid_out, attended)
```

```python
from functools import partial

import jax
import jax.numpy as jnp
from jax import lax
from jax.experimental import pallas as pl
from jax.experimental.pallas import tpu as pltpu
from jax.sharding import PartitionSpec as P

MODEL_WIDTH = 5376
HEAD_SIZE = 128
LONGEST_WINDOW = 1024


SCALE = 168.0 ** (-0.5)
EPS = 1e-06
THETA = 1000000.0
POSITION_FACTOR = 0.125


def shifted(value, axis, steps):
    count = lax.axis_size(axis)
    leading, last = (max(0, -steps), min(count, count - steps))
    return lax.ppermute(value, axis, [(source, source + steps) for source in range(leading, last)])


def from_partner(block, axis, bit):
    count = lax.axis_size(axis)
    route = []
    for low in range(count):
        high = low | 1 << bit
        if high != low and high < count:
            route += [(low, high), (high, low)]
    return lax.ppermute(block, axis, route)


def apply_rotary(values, pos_rows, factor):
    half_dim = values.shape[-1] // 2
    speeds = THETA ** (-(jnp.arange(half_dim, dtype=jnp.float32) * 2.0 / values.shape[-1]))
    angles = (pos_rows.astype(jnp.float32) * factor)[:, None] * speeds[None, :]
    cosine = jnp.cos(angles)[:, None, :]
    sine_part = jnp.sin(angles)[:, None, :]
    front_half = values[..., :half_dim]
    back_half = values[..., half_dim:]
    return jnp.concatenate(
        [front_half * cosine - back_half * sine_part, back_half * cosine + front_half * sine_part],
        axis=-1,
    )


def lookup(position_table, tokens):
    return jnp.take(position_table, jnp.clip(tokens, 0, position_table.shape[0] - 1))


def zig_token(row_ids, tok_dev):
    half_rows = tok_dev // 2
    device_of = row_ids // tok_dev
    local_row = row_ids % tok_dev
    last_pair = 2 * lax.axis_size("ctx") - 1
    return jnp.where(
        local_row < half_rows,
        2 * device_of * half_rows + local_row,
        (last_pair - 2 * device_of) * half_rows + local_row - half_rows,
    )


def masked_attention(
    query_row_block,
    key_row_block,
    value_row_block,
    query_tok,
    key_tok,
    query_pos,
    key_pos,
    window_limits,
):
    scores = (
        jnp.einsum(
            "qagd,kad->qagk", query_row_block, key_row_block, preferred_element_type=jnp.float32
        )
        * SCALE
    )
    distance = query_tok[:, None] - key_tok[None, :]
    base_ok = (
        (distance >= 0)
        & (key_tok[None, :] >= 0)
        & (query_pos[:, None] - key_pos[None, :] == distance)
    )
    visible = base_ok[:, None, None, :] & (
        distance[:, None, None, :] < window_limits[None, :, :, None]
    )
    row_peak = jnp.max(jnp.where(visible, scores, -1e30), axis=-1, keepdims=True)
    lifted = jnp.where(visible, jnp.exp(scores - row_peak), 0.0)
    row_total = jnp.sum(lifted, axis=-1)
    mixed = jnp.einsum(
        "qagk,kad->qagd",
        lifted.astype(jnp.bfloat16),
        value_row_block,
        preferred_element_type=jnp.float32,
    )
    return (mixed / row_total[..., None]).astype(jnp.bfloat16)


def mirror(rows_block, mover):
    half_rows = rows_block.shape[0] // 2
    travel = rows_block[half_rows:]
    bit_count = lax.axis_size("ctx").bit_length() - 1
    for bit_index in range(bit_count):
        travel = mover(travel, bit_index)
    return jnp.concatenate([rows_block[:half_rows], travel], axis=0)


def project(residual_rows, pre_gain, proj_query, key_projection, value_projection, row_pos):
    row_count = residual_rows.shape[0]
    widened = residual_rows.astype(jnp.float32)
    normalized_rows = (
        pre_gain[None, :]
        * widened
        * lax.rsqrt(jnp.mean(widened * widened, axis=1, keepdims=True) + EPS)
    ).astype(jnp.bfloat16)
    query_heads = proj_query.shape[1] // HEAD_SIZE
    pair_heads = key_projection.shape[1] // HEAD_SIZE
    second_layer_query = (
        apply_rotary(
            jnp.dot(
                normalized_rows,
                lax.all_gather(proj_query, "ctx", axis=0, tiled=True),
                preferred_element_type=jnp.float32,
            ).reshape(row_count, query_heads, HEAD_SIZE),
            row_pos,
            POSITION_FACTOR,
        )
        .astype(jnp.bfloat16)
        .reshape(row_count, query_heads * HEAD_SIZE)
    )
    second_layer_key = (
        apply_rotary(
            jnp.dot(
                normalized_rows,
                lax.all_gather(key_projection, "ctx", axis=0, tiled=True),
                preferred_element_type=jnp.float32,
            ).reshape(row_count, pair_heads, HEAD_SIZE),
            row_pos,
            POSITION_FACTOR,
        )
        .astype(jnp.bfloat16)
        .reshape(row_count, pair_heads * HEAD_SIZE)
    )
    second_layer_value = jnp.dot(
        normalized_rows,
        lax.all_gather(value_projection, "ctx", axis=0, tiled=True),
        preferred_element_type=jnp.float32,
    ).astype(jnp.bfloat16)
    return (second_layer_query, second_layer_key, second_layer_value)


def attend_block(
    state, query_row_block, key_block, value_block, query_tok, query_pos, block_tok, block_pos
):
    row_peak, row_total, weighted = state
    scores = (
        jnp.einsum("qagd,kad->qagk", query_row_block, key_block, preferred_element_type=jnp.float32)
        * SCALE
    )
    distance = query_tok[:, None] - block_tok[None, :]
    visible = (distance >= 0) & (query_pos[:, None] - block_pos[None, :] == distance)
    visible = visible[:, None, None, :]
    new_peak = jnp.maximum(row_peak, jnp.max(jnp.where(visible, scores, -1e30), axis=-1))
    lifted = jnp.where(visible, jnp.exp(scores - new_peak[..., None]), 0.0)
    shrink = jnp.exp(row_peak - new_peak)
    row_total = row_total * shrink + jnp.sum(lifted, axis=-1)
    weighted = weighted * shrink[..., None] + jnp.einsum(
        "qagk,kad->qagd",
        lifted.astype(jnp.bfloat16),
        value_block,
        preferred_element_type=jnp.float32,
    )
    return (new_peak, row_total, weighted)


def keep_state(state):
    return state


def shards(
    resid_in,
    first_layer_queries,
    first_layer_keys,
    first_layer_values,
    out_one,
    post_gain,
    pre_gain,
    proj_query,
    key_projection,
    value_projection,
    window,
    positions,
):
    tok_dev = resid_in.shape[0]
    col_width = resid_in.shape[1]
    ctx_place = lax.axis_index("ctx")
    head_place = lax.axis_index("heads")
    query_heads = first_layer_queries.shape[1] // HEAD_SIZE
    pair_heads = first_layer_keys.shape[1] // HEAD_SIZE
    group_length = query_heads // pair_heads
    window_limits = window.reshape(pair_heads, group_length)
    own_pairs = jnp.stack([first_layer_keys, first_layer_values])
    reach_count = LONGEST_WINDOW // tok_dev
    pieces = [own_pairs]
    for section in range(reach_count):
        pieces = [shifted(own_pairs, "ctx", section + 1)] + pieces
    extended = jnp.concatenate(pieces, axis=1)
    key_span = extended.shape[1]
    local_tok = ctx_place * tok_dev + jnp.arange(tok_dev, dtype=jnp.int32)
    key_tok = (ctx_place - reach_count) * tok_dev + jnp.arange(key_span, dtype=jnp.int32)
    attend_one = masked_attention(
        first_layer_queries.reshape(tok_dev, pair_heads, group_length, HEAD_SIZE),
        extended[0].reshape(key_span, pair_heads, HEAD_SIZE),
        extended[1].reshape(key_span, pair_heads, HEAD_SIZE),
        local_tok,
        key_tok,
        lookup(positions, local_tok),
        lookup(positions, key_tok),
        window_limits,
    )
    attend_one = attend_one.reshape(tok_dev, query_heads * HEAD_SIZE)
    partial_rows = jnp.dot(attend_one, out_one, preferred_element_type=jnp.float32)
    mirror_tok = zig_token(ctx_place * tok_dev + jnp.arange(tok_dev, dtype=jnp.int32), tok_dev)
    mirror_pos = lookup(positions, mirror_tok)
    shared = lax.psum_scatter(
        partial_rows.astype(jnp.bfloat16), "heads", scatter_dimension=1, tiled=True
    ).astype(jnp.float32)
    squares = lax.psum(jnp.sum(shared * shared, axis=1), "heads")
    post_scaled = shared * lax.rsqrt(squares[:, None] / MODEL_WIDTH + EPS)
    gain_slice = lax.dynamic_slice_in_dim(post_gain, head_place * col_width, col_width, 0)
    resid_out = (resid_in.astype(jnp.float32) + gain_slice[None, :] * post_scaled).astype(
        jnp.bfloat16
    )

    def move_resid(piece, bit_index):
        return from_partner(piece, "ctx", bit_index)

    relayed = mirror(resid_out, move_resid)
    residual_rows = lax.all_gather(relayed, "heads", axis=1, tiled=True)
    second_layer_query, second_layer_key, second_layer_value = project(
        residual_rows, pre_gain, proj_query, key_projection, value_projection, mirror_pos
    )
    half_rows = tok_dev // 2
    queries = second_layer_query.reshape(tok_dev, pair_heads, group_length, HEAD_SIZE)
    query_parts = (queries[:half_rows], queries[half_rows:])
    tok_parts = (mirror_tok[:half_rows], mirror_tok[half_rows:])
    pos_parts = (mirror_pos[:half_rows], mirror_pos[half_rows:])
    pair_two = jnp.stack([second_layer_key, second_layer_value])

    def empty_state():
        return (
            jnp.full((half_rows, pair_heads, group_length), -1e30, jnp.float32),
            jnp.zeros((half_rows, pair_heads, group_length), jnp.float32),
            jnp.zeros((half_rows, pair_heads, group_length, HEAD_SIZE), jnp.float32),
        )

    start_state = (empty_state(), empty_state())
    piece = lax.all_gather(pair_two, "ctx", axis=1, tiled=True)
    piece_rows = piece.shape[1]
    unit_rows = 2 * tok_dev
    unit_count = piece_rows // unit_rows

    def one_unit(index, state):
        offset = index * unit_rows
        unit_block = lax.dynamic_slice_in_dim(piece, offset, unit_rows, 1)
        current = list(state)
        for key_half in range(unit_rows // half_rows):
            key_block = unit_block[0, key_half * half_rows : (key_half + 1) * half_rows].reshape(
                half_rows, pair_heads, HEAD_SIZE
            )
            value_block = unit_block[1, key_half * half_rows : (key_half + 1) * half_rows].reshape(
                half_rows, pair_heads, HEAD_SIZE
            )
            key_row_block = offset + key_half * half_rows + jnp.arange(half_rows, dtype=jnp.int32)
            block_tok = zig_token(key_row_block, tok_dev)
            block_pos = lookup(positions, block_tok)
            earliest = jnp.min(block_tok)
            for query_half in range(2):
                work = partial(
                    attend_block,
                    query_row_block=query_parts[query_half],
                    key_block=key_block,
                    value_block=value_block,
                    query_tok=tok_parts[query_half],
                    query_pos=pos_parts[query_half],
                    block_tok=block_tok,
                    block_pos=block_pos,
                )
                needed = earliest <= tok_parts[query_half][half_rows - 1]
                current[query_half] = lax.cond(needed, work, keep_state, current[query_half])
        return tuple(current)

    final_state = lax.fori_loop(0, unit_count, one_unit, start_state)
    front = final_state[0][2] / final_state[0][1][..., None]
    back = final_state[1][2] / final_state[1][1][..., None]
    attended = (
        jnp.concatenate([front, back], axis=0)
        .astype(jnp.bfloat16)
        .reshape(tok_dev, query_heads * HEAD_SIZE)
    )
    return (resid_out, attended)


MESH = pl.DeviceIdType.MESH
QUERY_TILE = 256


def spread_fits(mesh):
    return mesh.shape["heads"] == 2 and mesh.shape["ctx"] == 16


def greet_all(count):
    me, core = lax.axis_index("ctx"), lax.axis_index("heads")
    barrier = pltpu.get_barrier_semaphore()

    def greet(step, carry):
        pl.semaphore_signal(
            barrier, inc=1, device_id=(lax.rem(me + step, count), core), device_id_type=MESH
        )
        pl.semaphore_signal(
            barrier, inc=1, device_id=(lax.rem(me + step, count), 1 - core), device_id_type=MESH
        )
        return carry

    lax.fori_loop(1, count, greet, 0)
    pl.semaphore_signal(barrier, inc=1, device_id=(me, 1 - core), device_id_type=MESH)
    pl.semaphore_wait(barrier, 2 * count - 1)


def attend_tile(tile, band, query_ref, key_ref, value_ref, low_ref, mixed_ref):
    tokens = query_ref.shape[0]
    span = min(band + QUERY_TILE, tokens)
    first = pl.multiple_of(tile * QUERY_TILE, QUERY_TILE)
    begin = pl.multiple_of(jnp.maximum(first + QUERY_TILE - span, 0), QUERY_TILE)
    scores = (
        lax.dot_general(
            query_ref[pl.ds(first, QUERY_TILE), :],
            key_ref[pl.ds(begin, span), :],
            (((1,), (1,)), ((), ())),
            preferred_element_type=jnp.float32,
        )
        * SCALE
    )
    rows = first + lax.broadcasted_iota(jnp.int32, (QUERY_TILE, 1), 0)
    columns = begin + lax.broadcasted_iota(jnp.int32, (1, span), 1)
    visible = (columns <= rows) & (columns >= low_ref[pl.ds(first, QUERY_TILE), :])
    scores = jnp.where(visible, scores, -1e30)
    lifted = jnp.exp(scores - jnp.max(scores, axis=1, keepdims=True))
    total = jnp.sum(lifted, axis=1, keepdims=True)
    mixed = jnp.dot(
        lifted.astype(jnp.bfloat16),
        value_ref[pl.ds(begin, span), :],
        preferred_element_type=jnp.float32,
    )
    mixed_ref[pl.ds(first, QUERY_TILE), :] = (mixed / total).astype(jnp.bfloat16)


def first_kernel(
    count,
    band,
    query_in,
    key_in,
    value_in,
    low_ref,
    wq_ref,
    wk_ref,
    wv_ref,
    attend_out,
    weight_out,
    query_all,
    key_all,
    value_all,
    mixed,
    in_send,
    in_recv,
    in_own,
    back_send,
    back_recv,
    back_own,
    w_send,
    w_recv,
    w_own,
):
    me, core = lax.axis_index("ctx"), lax.axis_index("heads")
    tok = query_in.shape[0]
    depth = wq_ref.shape[0]
    half = count // 2
    greet_all(count)

    def columns(index):
        return pl.ds(pl.multiple_of(index * HEAD_SIZE, HEAD_SIZE), HEAD_SIZE)

    def rows(index, size=tok):
        return pl.ds(pl.multiple_of(index * size, size), size)

    def inward(step):
        to = lax.rem(me + step, count)
        trio = (
            (query_in, query_all, to),
            (key_in, key_all, to // 2),
            (value_in, value_all, to // 2),
        )
        return [
            pltpu.make_async_remote_copy(
                src_ref=source.at[:, columns(block)],
                dst_ref=target.at[rows(me), :],
                send_sem=in_send.at[kind, step],
                recv_sem=in_recv.at[kind, step],
                device_id=(to, core),
                device_id_type=MESH,
            )
            for kind, (source, target, block) in enumerate(trio)
        ]

    def start_inward(step, carry):
        for copy in inward(step):
            copy.start()
        return carry

    def wait_inward(step, carry):
        for copy in inward(step):
            copy.wait()
        return carry

    lax.fori_loop(1, count, start_inward, 0)
    own = [
        pltpu.make_async_copy(source.at[:, columns(block)], target.at[rows(me), :], in_own.at[kind])
        for kind, (source, target, block) in enumerate(
            (
                (query_in, query_all, me),
                (key_in, key_all, me // 2),
                (value_in, value_all, me // 2),
            )
        )
    ]
    for copy in own:
        copy.start()
    for copy in own:
        copy.wait()
    lax.fori_loop(1, count, wait_inward, 0)

    to_core = me // half
    place = lax.rem(me, half)
    apart = jnp.where(to_core == core, 0, 1)

    def weight_views(pair, odd):
        to = 2 * pair + odd
        base = pl.multiple_of(apart * 2 * HEAD_SIZE, HEAD_SIZE)
        next_base = pl.multiple_of(apart * 2 * HEAD_SIZE + HEAD_SIZE, HEAD_SIZE)
        second = wk_ref if odd == 0 else wv_ref
        return (
            (wq_ref.at[:, columns(to)], weight_out.at[rows(place, depth), pl.ds(base, HEAD_SIZE)]),
            (
                second.at[:, columns(pair)],
                weight_out.at[rows(place, depth), pl.ds(next_base, HEAD_SIZE)],
            ),
        )

    def weight_remote(pair, odd):
        to = 2 * pair + odd
        return [
            pltpu.make_async_remote_copy(
                src_ref=source,
                dst_ref=target,
                send_sem=w_send.at[kind, to],
                recv_sem=w_recv.at[kind, place * 2 + apart],
                device_id=(to, to_core),
                device_id_type=MESH,
            )
            for kind, (source, target) in enumerate(weight_views(pair, odd))
        ]

    def weight_local(pair, odd):
        return [
            pltpu.make_async_copy(source, target, w_own.at[kind])
            for kind, (source, target) in enumerate(weight_views(pair, odd))
        ]

    def each_weight(act_remote, act_local):
        def body(pair, carry):
            for odd in range(2):
                to = 2 * pair + odd
                mine = (to == me) & (to_core == core)

                @pl.when(jnp.logical_not(mine))
                def _():
                    for copy in weight_remote(pair, odd):
                        act_remote(copy)

                @pl.when(mine)
                def _():
                    for copy in weight_local(pair, odd):
                        act_local(copy)

            return carry

        lax.fori_loop(0, half, body, 0)

    each_weight(lambda copy: copy.start(), lambda copy: copy.start())

    def outward(to):
        return pltpu.make_async_remote_copy(
            src_ref=mixed.at[rows(to), :],
            dst_ref=attend_out.at[:, columns(me)],
            send_sem=back_send.at[to],
            recv_sem=back_recv.at[me],
            device_id=(to, core),
            device_id_type=MESH,
        )

    def outward_own():
        return pltpu.make_async_copy(
            mixed.at[rows(me), :], attend_out.at[:, columns(me)], back_own
        )

    per_tile = QUERY_TILE // tok

    def one_tile(tile, carry):
        attend_tile(tile, band, query_all, key_all, value_all, low_ref, mixed)
        for part in range(per_tile):
            to = tile * per_tile + part

            @pl.when(to != me)
            def _():
                outward(to).start()

            @pl.when(to == me)
            def _():
                outward_own().start()

        return carry

    lax.fori_loop(0, count // per_tile, one_tile, 0)

    def finish(step, carry):
        to = lax.rem(me + step, count)
        outward(to).wait_send()
        pltpu.make_async_remote_copy(
            src_ref=mixed.at[rows(to), :],
            dst_ref=attend_out.at[:, columns(to)],
            send_sem=back_send.at[to],
            recv_sem=back_recv.at[to],
            device_id=(to, core),
            device_id_type=MESH,
        ).wait_recv()
        return carry

    lax.fori_loop(1, count, finish, 0)
    outward_own().wait()
    each_weight(lambda copy: copy.wait_send(), lambda copy: copy.wait())

    def weight_arrived(slot, carry):
        from_place, from_apart = slot // 2, lax.rem(slot, 2)
        sender = core * half + from_place
        mine = (sender == me) & (from_apart == 0)

        @pl.when(jnp.logical_not(mine))
        def _():
            for kind in range(2):
                left = pl.multiple_of((from_apart * 2 + kind) * HEAD_SIZE, HEAD_SIZE)
                view = weight_out.at[rows(from_place, depth), pl.ds(left, HEAD_SIZE)]
                pltpu.make_async_remote_copy(
                    src_ref=view,
                    dst_ref=view,
                    send_sem=w_send.at[kind, 0],
                    recv_sem=w_recv.at[kind, slot],
                    device_id=(me, 1 - core),
                    device_id_type=MESH,
                ).wait_recv()

        return carry

    lax.fori_loop(0, count, weight_arrived, 0)


def first_attention(count, band, queries, keys, values, low, wq, wk, wv):
    tok = queries.shape[0]
    tokens = tok * count
    whole = (tokens, HEAD_SIZE)
    dma = pltpu.SemaphoreType.DMA
    vmem = pl.BlockSpec(memory_space=pltpu.VMEM)
    anywhere = pl.BlockSpec(memory_space=pl.ANY)
    return pl.pallas_call(
        partial(first_kernel, count, band),
        out_shape=(
            jax.ShapeDtypeStruct(queries.shape, jnp.bfloat16),
            jax.ShapeDtypeStruct((wq.shape[0] * count // 2, 4 * HEAD_SIZE), jnp.bfloat16),
        ),
        in_specs=[vmem] * 4 + [anywhere] * 3,
        out_specs=(anywhere, anywhere),
        scratch_shapes=[pltpu.VMEM(whole, jnp.bfloat16)] * 4
        + [
            dma((3, count)),
            dma((3, count)),
            dma((3,)),
            dma((count,)),
            dma((count,)),
            dma,
            dma((2, count)),
            dma((2, count)),
            dma((2,)),
        ],
        compiler_params=pltpu.CompilerParams(
            collective_id=0, has_side_effects=True, vmem_limit_bytes=48 * 1024 * 1024
        ),
        name="first_attention",
    )(queries, keys, values, low, wq, wk, wv)


def second_kernel(
    count, band, query_ref, key_ref, value_ref, low_ref, attend_out, mixed, back_send, back_recv, back_own
):
    me, core = lax.axis_index("ctx"), lax.axis_index("heads")
    half = attend_out.shape[0] // 2
    blocks = 2 * count
    greet_all(count)
    own_columns = pl.ds(pl.multiple_of(me * HEAD_SIZE, HEAD_SIZE), HEAD_SIZE)

    def home(block):
        odd = lax.rem(block, 2)
        return jnp.where(odd == 0, block // 2, (blocks - 1 - block) // 2), odd

    def rows(index):
        return pl.ds(pl.multiple_of(index * half, half), half)

    def outward(block, to, odd):
        return pltpu.make_async_remote_copy(
            src_ref=mixed.at[rows(block), :],
            dst_ref=attend_out.at[rows(odd), own_columns],
            send_sem=back_send.at[block],
            recv_sem=back_recv.at[odd, me],
            device_id=(to, core),
            device_id_type=MESH,
        )

    def outward_own(block, odd):
        return pltpu.make_async_copy(
            mixed.at[rows(block), :], attend_out.at[rows(odd), own_columns], back_own.at[odd]
        )

    per_tile = QUERY_TILE // half

    def one_tile(tile, carry):
        attend_tile(tile, band, query_ref, key_ref, value_ref, low_ref, mixed)
        for part in range(per_tile):
            block = tile * per_tile + part
            to, odd = home(block)

            @pl.when(to != me)
            def _():
                outward(block, to, odd).start()

            @pl.when(to == me)
            def _():
                outward_own(block, odd).start()

        return carry

    lax.fori_loop(0, blocks // per_tile, one_tile, 0)

    def finish(block, carry):
        to, odd = home(block)

        @pl.when(to != me)
        def _():
            outward(block, to, odd).wait_send()

        @pl.when(to == me)
        def _():
            outward_own(block, odd).wait()

        return carry

    lax.fori_loop(0, blocks, finish, 0)

    def arrived(step, carry):
        sender = lax.rem(me + step, count)
        left = pl.multiple_of(sender * HEAD_SIZE, HEAD_SIZE)
        for odd in range(2):
            view = attend_out.at[pl.ds(odd * half, half), pl.ds(left, HEAD_SIZE)]
            pltpu.make_async_remote_copy(
                src_ref=view,
                dst_ref=view,
                send_sem=back_send.at[0],
                recv_sem=back_recv.at[odd, sender],
                device_id=(sender, core),
                device_id_type=MESH,
            ).wait_recv()
        return carry

    lax.fori_loop(1, count, arrived, 0)


def second_attention(count, band, queries, keys, values, low):
    tokens = queries.shape[0]
    dma = pltpu.SemaphoreType.DMA
    vmem = pl.BlockSpec(memory_space=pltpu.VMEM)
    return pl.pallas_call(
        partial(second_kernel, count, band),
        out_shape=jax.ShapeDtypeStruct((tokens // count, count * HEAD_SIZE), jnp.bfloat16),
        in_specs=[vmem] * 4,
        out_specs=pl.BlockSpec(memory_space=pl.ANY),
        scratch_shapes=[
            pltpu.VMEM((tokens, HEAD_SIZE), jnp.bfloat16),
            dma((2 * count,)),
            dma((2, count)),
            dma((2,)),
        ],
        compiler_params=pltpu.CompilerParams(
            collective_id=1, has_side_effects=True, vmem_limit_bytes=48 * 1024 * 1024
        ),
        name="second_attention",
    )(queries, keys, values, low)


def to_other_core(block):
    return lax.ppermute(block, "heads", [(0, 1), (1, 0)])


def shards_by_head(
    count,
    resid_in,
    first_layer_queries,
    first_layer_keys,
    first_layer_values,
    out_one,
    post_gain,
    pre_gain,
    proj_query,
    key_projection,
    value_projection,
    window,
    positions,
):
    me, core = lax.axis_index("ctx"), lax.axis_index("heads")
    col_width = resid_in.shape[1]
    tokens = positions.shape[0]
    token = jnp.arange(tokens, dtype=jnp.int32)
    document = token - positions
    own_window = lax.dynamic_index_in_dim(window, me, 0, keepdims=False)
    low_one = jnp.maximum(document, token - own_window + 1)
    resid_other = to_other_core(resid_in)
    attend_one, weights = first_attention(
        count,
        LONGEST_WINDOW,
        first_layer_queries,
        first_layer_keys,
        first_layer_values,
        low_one[:, None],
        proj_query,
        key_projection,
        value_projection,
    )
    partial_rows = jnp.dot(attend_one, out_one, preferred_element_type=jnp.float32).astype(
        jnp.bfloat16
    )
    combined = partial_rows.astype(jnp.float32) + to_other_core(partial_rows).astype(jnp.float32)
    post_scaled = combined * lax.rsqrt(
        jnp.mean(combined * combined, axis=1, keepdims=True) + EPS
    )
    resid_row = jnp.where(
        core == 0,
        jnp.concatenate([resid_in, resid_other], axis=1),
        jnp.concatenate([resid_other, resid_in], axis=1),
    )
    resid_full = (resid_row.astype(jnp.float32) + post_gain[None, :] * post_scaled).astype(
        jnp.bfloat16
    )
    resid_out = lax.dynamic_slice_in_dim(resid_full, core * col_width, col_width, 1)
    widened = resid_full.astype(jnp.float32)
    factor = lax.rsqrt(jnp.mean(widened * widened, axis=1, keepdims=True) + EPS)
    gain_slice = lax.dynamic_slice_in_dim(pre_gain, core * col_width, col_width, 0)
    normed = (gain_slice[None, :] * resid_out.astype(jnp.float32) * factor).astype(jnp.bfloat16)
    gathered = lax.all_gather(normed, "ctx", axis=0, tiled=True)
    away = jnp.dot(gathered, weights[:, 2 * HEAD_SIZE :], preferred_element_type=jnp.float32)
    arrived = to_other_core(away)
    kept = jnp.dot(gathered, weights[:, : 2 * HEAD_SIZE], preferred_element_type=jnp.float32)
    product = (kept + arrived).reshape(tokens, 2, HEAD_SIZE)
    rotated = apply_rotary(product, positions, POSITION_FACTOR).astype(jnp.bfloat16)
    even = lax.rem(me, 2) == 0
    query_two = rotated[:, 0]
    mine = jnp.where(even, rotated[:, 1], product[:, 1].astype(jnp.bfloat16))
    theirs = from_partner(mine, "ctx", 0)
    key_two = jnp.where(even, mine, theirs)
    value_two = jnp.where(even, theirs, mine)
    attended = second_attention(
        count, tokens // 2, query_two, key_two, value_two, document[:, None]
    )
    return (resid_out, attended)


def solution(mesh):
    placed = (
        P("ctx", "heads"),
        P("ctx", "heads"),
        P("ctx", "heads"),
        P("ctx", "heads"),
        P("heads", None),
        P(),
        P(),
        P("ctx", "heads"),
        P("ctx", "heads"),
        P("ctx", "heads"),
        P("heads"),
        P(),
    )
    return jax.shard_map(
        partial(shards_by_head, mesh.shape["ctx"])
        if spread_fits(mesh)
        else shards,
        mesh=mesh,
        in_specs=placed,
        out_specs=(P("ctx", "heads"), P("ctx", "heads")),
        check_vma=False,
    )
```

```python
from functools import partial

import jax
import jax.numpy as jnp
from jax import lax
from jax.experimental import pallas as pl
from jax.experimental.pallas import tpu as pltpu
from jax.sharding import PartitionSpec as P

MODEL_WIDTH = 5376
HEAD_SIZE = 128
LONGEST_WINDOW = 1024


SCALE = 168.0 ** (-0.5)
EPS = 1e-06
THETA = 1000000.0
POSITION_FACTOR = 0.125


def shifted(value, axis, steps):
    count = lax.axis_size(axis)
    leading, last = (max(0, -steps), min(count, count - steps))
    return lax.ppermute(value, axis, [(source, source + steps) for source in range(leading, last)])


def from_partner(block, axis, bit):
    count = lax.axis_size(axis)
    route = []
    for low in range(count):
        high = low | 1 << bit
        if high != low and high < count:
            route += [(low, high), (high, low)]
    return lax.ppermute(block, axis, route)


def apply_rotary(values, pos_rows, factor):
    half_dim = values.shape[-1] // 2
    speeds = THETA ** (-(jnp.arange(half_dim, dtype=jnp.float32) * 2.0 / values.shape[-1]))
    angles = (pos_rows.astype(jnp.float32) * factor)[:, None] * speeds[None, :]
    cosine = jnp.cos(angles)[:, None, :]
    sine_part = jnp.sin(angles)[:, None, :]
    front_half = values[..., :half_dim]
    back_half = values[..., half_dim:]
    return jnp.concatenate(
        [front_half * cosine - back_half * sine_part, back_half * cosine + front_half * sine_part],
        axis=-1,
    )


def lookup(position_table, tokens):
    return jnp.take(position_table, jnp.clip(tokens, 0, position_table.shape[0] - 1))


def zig_token(row_ids, tok_dev):
    half_rows = tok_dev // 2
    device_of = row_ids // tok_dev
    local_row = row_ids % tok_dev
    last_pair = 2 * lax.axis_size("ctx") - 1
    return jnp.where(
        local_row < half_rows,
        2 * device_of * half_rows + local_row,
        (last_pair - 2 * device_of) * half_rows + local_row - half_rows,
    )


def masked_attention(
    query_row_block,
    key_row_block,
    value_row_block,
    query_tok,
    key_tok,
    query_pos,
    key_pos,
    window_limits,
):
    scores = (
        jnp.einsum(
            "qagd,kad->qagk", query_row_block, key_row_block, preferred_element_type=jnp.float32
        )
        * SCALE
    )
    distance = query_tok[:, None] - key_tok[None, :]
    base_ok = (
        (distance >= 0)
        & (key_tok[None, :] >= 0)
        & (query_pos[:, None] - key_pos[None, :] == distance)
    )
    visible = base_ok[:, None, None, :] & (
        distance[:, None, None, :] < window_limits[None, :, :, None]
    )
    row_peak = jnp.max(jnp.where(visible, scores, -1e30), axis=-1, keepdims=True)
    lifted = jnp.where(visible, jnp.exp(scores - row_peak), 0.0)
    row_total = jnp.sum(lifted, axis=-1)
    mixed = jnp.einsum(
        "qagk,kad->qagd",
        lifted.astype(jnp.bfloat16),
        value_row_block,
        preferred_element_type=jnp.float32,
    )
    return (mixed / row_total[..., None]).astype(jnp.bfloat16)


def mirror(rows_block, mover):
    half_rows = rows_block.shape[0] // 2
    travel = rows_block[half_rows:]
    bit_count = lax.axis_size("ctx").bit_length() - 1
    for bit_index in range(bit_count):
        travel = mover(travel, bit_index)
    return jnp.concatenate([rows_block[:half_rows], travel], axis=0)


def project(residual_rows, pre_gain, proj_query, key_projection, value_projection, row_pos):
    row_count = residual_rows.shape[0]
    widened = residual_rows.astype(jnp.float32)
    normalized_rows = (
        pre_gain[None, :]
        * widened
        * lax.rsqrt(jnp.mean(widened * widened, axis=1, keepdims=True) + EPS)
    ).astype(jnp.bfloat16)
    query_heads = proj_query.shape[1] // HEAD_SIZE
    pair_heads = key_projection.shape[1] // HEAD_SIZE
    second_layer_query = (
        apply_rotary(
            jnp.dot(
                normalized_rows,
                lax.all_gather(proj_query, "ctx", axis=0, tiled=True),
                preferred_element_type=jnp.float32,
            ).reshape(row_count, query_heads, HEAD_SIZE),
            row_pos,
            POSITION_FACTOR,
        )
        .astype(jnp.bfloat16)
        .reshape(row_count, query_heads * HEAD_SIZE)
    )
    second_layer_key = (
        apply_rotary(
            jnp.dot(
                normalized_rows,
                lax.all_gather(key_projection, "ctx", axis=0, tiled=True),
                preferred_element_type=jnp.float32,
            ).reshape(row_count, pair_heads, HEAD_SIZE),
            row_pos,
            POSITION_FACTOR,
        )
        .astype(jnp.bfloat16)
        .reshape(row_count, pair_heads * HEAD_SIZE)
    )
    second_layer_value = jnp.dot(
        normalized_rows,
        lax.all_gather(value_projection, "ctx", axis=0, tiled=True),
        preferred_element_type=jnp.float32,
    ).astype(jnp.bfloat16)
    return (second_layer_query, second_layer_key, second_layer_value)


def attend_block(
    state, query_row_block, key_block, value_block, query_tok, query_pos, block_tok, block_pos
):
    row_peak, row_total, weighted = state
    scores = (
        jnp.einsum("qagd,kad->qagk", query_row_block, key_block, preferred_element_type=jnp.float32)
        * SCALE
    )
    distance = query_tok[:, None] - block_tok[None, :]
    visible = (distance >= 0) & (query_pos[:, None] - block_pos[None, :] == distance)
    visible = visible[:, None, None, :]
    new_peak = jnp.maximum(row_peak, jnp.max(jnp.where(visible, scores, -1e30), axis=-1))
    lifted = jnp.where(visible, jnp.exp(scores - new_peak[..., None]), 0.0)
    shrink = jnp.exp(row_peak - new_peak)
    row_total = row_total * shrink + jnp.sum(lifted, axis=-1)
    weighted = weighted * shrink[..., None] + jnp.einsum(
        "qagk,kad->qagd",
        lifted.astype(jnp.bfloat16),
        value_block,
        preferred_element_type=jnp.float32,
    )
    return (new_peak, row_total, weighted)


def keep_state(state):
    return state


def shards(
    resid_in,
    first_layer_queries,
    first_layer_keys,
    first_layer_values,
    out_one,
    post_gain,
    pre_gain,
    proj_query,
    key_projection,
    value_projection,
    window,
    positions,
):
    tok_dev = resid_in.shape[0]
    col_width = resid_in.shape[1]
    ctx_place = lax.axis_index("ctx")
    head_place = lax.axis_index("heads")
    query_heads = first_layer_queries.shape[1] // HEAD_SIZE
    pair_heads = first_layer_keys.shape[1] // HEAD_SIZE
    group_length = query_heads // pair_heads
    window_limits = window.reshape(pair_heads, group_length)
    own_pairs = jnp.stack([first_layer_keys, first_layer_values])
    reach_count = LONGEST_WINDOW // tok_dev
    pieces = [own_pairs]
    for section in range(reach_count):
        pieces = [shifted(own_pairs, "ctx", section + 1)] + pieces
    extended = jnp.concatenate(pieces, axis=1)
    key_span = extended.shape[1]
    local_tok = ctx_place * tok_dev + jnp.arange(tok_dev, dtype=jnp.int32)
    key_tok = (ctx_place - reach_count) * tok_dev + jnp.arange(key_span, dtype=jnp.int32)
    attend_one = masked_attention(
        first_layer_queries.reshape(tok_dev, pair_heads, group_length, HEAD_SIZE),
        extended[0].reshape(key_span, pair_heads, HEAD_SIZE),
        extended[1].reshape(key_span, pair_heads, HEAD_SIZE),
        local_tok,
        key_tok,
        lookup(positions, local_tok),
        lookup(positions, key_tok),
        window_limits,
    )
    attend_one = attend_one.reshape(tok_dev, query_heads * HEAD_SIZE)
    partial_rows = jnp.dot(attend_one, out_one, preferred_element_type=jnp.float32)
    mirror_tok = zig_token(ctx_place * tok_dev + jnp.arange(tok_dev, dtype=jnp.int32), tok_dev)
    mirror_pos = lookup(positions, mirror_tok)
    shared = lax.psum_scatter(
        partial_rows.astype(jnp.bfloat16), "heads", scatter_dimension=1, tiled=True
    ).astype(jnp.float32)
    squares = lax.psum(jnp.sum(shared * shared, axis=1), "heads")
    post_scaled = shared * lax.rsqrt(squares[:, None] / MODEL_WIDTH + EPS)
    gain_slice = lax.dynamic_slice_in_dim(post_gain, head_place * col_width, col_width, 0)
    resid_out = (resid_in.astype(jnp.float32) + gain_slice[None, :] * post_scaled).astype(
        jnp.bfloat16
    )

    def move_resid(piece, bit_index):
        return from_partner(piece, "ctx", bit_index)

    relayed = mirror(resid_out, move_resid)
    residual_rows = lax.all_gather(relayed, "heads", axis=1, tiled=True)
    second_layer_query, second_layer_key, second_layer_value = project(
        residual_rows, pre_gain, proj_query, key_projection, value_projection, mirror_pos
    )
    half_rows = tok_dev // 2
    queries = second_layer_query.reshape(tok_dev, pair_heads, group_length, HEAD_SIZE)
    query_parts = (queries[:half_rows], queries[half_rows:])
    tok_parts = (mirror_tok[:half_rows], mirror_tok[half_rows:])
    pos_parts = (mirror_pos[:half_rows], mirror_pos[half_rows:])
    pair_two = jnp.stack([second_layer_key, second_layer_value])

    def empty_state():
        return (
            jnp.full((half_rows, pair_heads, group_length), -1e30, jnp.float32),
            jnp.zeros((half_rows, pair_heads, group_length), jnp.float32),
            jnp.zeros((half_rows, pair_heads, group_length, HEAD_SIZE), jnp.float32),
        )

    start_state = (empty_state(), empty_state())
    piece = lax.all_gather(pair_two, "ctx", axis=1, tiled=True)
    piece_rows = piece.shape[1]
    unit_rows = 2 * tok_dev
    unit_count = piece_rows // unit_rows

    def one_unit(index, state):
        offset = index * unit_rows
        unit_block = lax.dynamic_slice_in_dim(piece, offset, unit_rows, 1)
        current = list(state)
        for key_half in range(unit_rows // half_rows):
            key_block = unit_block[0, key_half * half_rows : (key_half + 1) * half_rows].reshape(
                half_rows, pair_heads, HEAD_SIZE
            )
            value_block = unit_block[1, key_half * half_rows : (key_half + 1) * half_rows].reshape(
                half_rows, pair_heads, HEAD_SIZE
            )
            key_row_block = offset + key_half * half_rows + jnp.arange(half_rows, dtype=jnp.int32)
            block_tok = zig_token(key_row_block, tok_dev)
            block_pos = lookup(positions, block_tok)
            earliest = jnp.min(block_tok)
            for query_half in range(2):
                work = partial(
                    attend_block,
                    query_row_block=query_parts[query_half],
                    key_block=key_block,
                    value_block=value_block,
                    query_tok=tok_parts[query_half],
                    query_pos=pos_parts[query_half],
                    block_tok=block_tok,
                    block_pos=block_pos,
                )
                needed = earliest <= tok_parts[query_half][half_rows - 1]
                current[query_half] = lax.cond(needed, work, keep_state, current[query_half])
        return tuple(current)

    final_state = lax.fori_loop(0, unit_count, one_unit, start_state)
    front = final_state[0][2] / final_state[0][1][..., None]
    back = final_state[1][2] / final_state[1][1][..., None]
    attended = (
        jnp.concatenate([front, back], axis=0)
        .astype(jnp.bfloat16)
        .reshape(tok_dev, query_heads * HEAD_SIZE)
    )
    return (resid_out, attended)


MESH = pl.DeviceIdType.MESH
QUERY_TILE = 256


def spread_fits(mesh):
    return mesh.shape["heads"] == 2 and mesh.shape["ctx"] == 16


def greet_all(count):
    me, core = lax.axis_index("ctx"), lax.axis_index("heads")
    barrier = pltpu.get_barrier_semaphore()

    def greet(step, carry):
        pl.semaphore_signal(
            barrier, inc=1, device_id=(lax.rem(me + step, count), core), device_id_type=MESH
        )
        pl.semaphore_signal(
            barrier, inc=1, device_id=(lax.rem(me + step, count), 1 - core), device_id_type=MESH
        )
        return carry

    lax.fori_loop(1, count, greet, 0)
    pl.semaphore_signal(barrier, inc=1, device_id=(me, 1 - core), device_id_type=MESH)
    pl.semaphore_wait(barrier, 2 * count - 1)


def attend_tile(tile, band, query_ref, key_ref, value_ref, low_ref, mixed_ref):
    tokens = query_ref.shape[0]
    span = min(band + QUERY_TILE, tokens)
    first = pl.multiple_of(tile * QUERY_TILE, QUERY_TILE)
    begin = pl.multiple_of(jnp.maximum(first + QUERY_TILE - span, 0), QUERY_TILE)
    scores = (
        lax.dot_general(
            query_ref[pl.ds(first, QUERY_TILE), :],
            key_ref[pl.ds(begin, span), :],
            (((1,), (1,)), ((), ())),
            preferred_element_type=jnp.float32,
        )
        * SCALE
    )
    rows = first + lax.broadcasted_iota(jnp.int32, (QUERY_TILE, 1), 0)
    columns = begin + lax.broadcasted_iota(jnp.int32, (1, span), 1)
    visible = (columns <= rows) & (columns >= low_ref[pl.ds(first, QUERY_TILE), :])
    scores = jnp.where(visible, scores, -1e30)
    lifted = jnp.exp(scores - jnp.max(scores, axis=1, keepdims=True))
    total = jnp.sum(lifted, axis=1, keepdims=True)
    mixed = jnp.dot(
        lifted.astype(jnp.bfloat16),
        value_ref[pl.ds(begin, span), :],
        preferred_element_type=jnp.float32,
    )
    mixed_ref[pl.ds(first, QUERY_TILE), :] = (mixed / total).astype(jnp.bfloat16)


def first_kernel(
    count,
    band,
    query_in,
    key_in,
    value_in,
    low_ref,
    wq_ref,
    wk_ref,
    wv_ref,
    attend_out,
    weight_out,
    query_all,
    key_all,
    value_all,
    mixed,
    in_send,
    in_recv,
    in_own,
    back_send,
    back_recv,
    back_own,
    w_send,
    w_recv,
    w_own,
):
    me, core = lax.axis_index("ctx"), lax.axis_index("heads")
    tok = query_in.shape[0]
    depth = wq_ref.shape[0]
    half = count // 2
    greet_all(count)

    def columns(index):
        return pl.ds(pl.multiple_of(index * HEAD_SIZE, HEAD_SIZE), HEAD_SIZE)

    def rows(index, size=tok):
        return pl.ds(pl.multiple_of(index * size, size), size)

    def inward(step):
        to = lax.rem(me + step, count)
        trio = (
            (query_in, query_all, to),
            (key_in, key_all, to // 2),
            (value_in, value_all, to // 2),
        )
        return [
            pltpu.make_async_remote_copy(
                src_ref=source.at[:, columns(block)],
                dst_ref=target.at[rows(me), :],
                send_sem=in_send.at[kind, step],
                recv_sem=in_recv.at[kind, step],
                device_id=(to, core),
                device_id_type=MESH,
            )
            for kind, (source, target, block) in enumerate(trio)
        ]

    def start_inward(step, carry):
        for copy in inward(step):
            copy.start()
        return carry

    def wait_inward(step, carry):
        for copy in inward(step):
            copy.wait()
        return carry

    lax.fori_loop(1, count, start_inward, 0)
    own = [
        pltpu.make_async_copy(source.at[:, columns(block)], target.at[rows(me), :], in_own.at[kind])
        for kind, (source, target, block) in enumerate(
            (
                (query_in, query_all, me),
                (key_in, key_all, me // 2),
                (value_in, value_all, me // 2),
            )
        )
    ]
    for copy in own:
        copy.start()
    for copy in own:
        copy.wait()
    lax.fori_loop(1, count, wait_inward, 0)

    to_core = me // half
    place = lax.rem(me, half)
    apart = jnp.where(to_core == core, 0, 1)

    def weight_views(pair, odd):
        to = 2 * pair + odd
        base = pl.multiple_of(apart * 2 * HEAD_SIZE, HEAD_SIZE)
        next_base = pl.multiple_of(apart * 2 * HEAD_SIZE + HEAD_SIZE, HEAD_SIZE)
        second = wk_ref if odd == 0 else wv_ref
        return (
            (wq_ref.at[:, columns(to)], weight_out.at[rows(place, depth), pl.ds(base, HEAD_SIZE)]),
            (
                second.at[:, columns(pair)],
                weight_out.at[rows(place, depth), pl.ds(next_base, HEAD_SIZE)],
            ),
        )

    def weight_remote(pair, odd):
        to = 2 * pair + odd
        return [
            pltpu.make_async_remote_copy(
                src_ref=source,
                dst_ref=target,
                send_sem=w_send.at[kind, to],
                recv_sem=w_recv.at[kind, place * 2 + apart],
                device_id=(to, to_core),
                device_id_type=MESH,
            )
            for kind, (source, target) in enumerate(weight_views(pair, odd))
        ]

    def weight_local(pair, odd):
        return [
            pltpu.make_async_copy(source, target, w_own.at[kind])
            for kind, (source, target) in enumerate(weight_views(pair, odd))
        ]

    def each_weight(act_remote, act_local):
        def body(pair, carry):
            for odd in range(2):
                to = 2 * pair + odd
                mine = (to == me) & (to_core == core)

                @pl.when(jnp.logical_not(mine))
                def _():
                    for copy in weight_remote(pair, odd):
                        act_remote(copy)

                @pl.when(mine)
                def _():
                    for copy in weight_local(pair, odd):
                        act_local(copy)

            return carry

        lax.fori_loop(0, half, body, 0)

    each_weight(lambda copy: copy.start(), lambda copy: copy.start())

    def outward(to):
        return pltpu.make_async_remote_copy(
            src_ref=mixed.at[rows(to), :],
            dst_ref=attend_out.at[:, columns(me)],
            send_sem=back_send.at[to],
            recv_sem=back_recv.at[me],
            device_id=(to, core),
            device_id_type=MESH,
        )

    def outward_own():
        return pltpu.make_async_copy(
            mixed.at[rows(me), :], attend_out.at[:, columns(me)], back_own
        )

    per_tile = QUERY_TILE // tok

    def one_tile(tile, carry):
        attend_tile(tile, band, query_all, key_all, value_all, low_ref, mixed)
        for part in range(per_tile):
            to = tile * per_tile + part

            @pl.when(to != me)
            def _():
                outward(to).start()

            @pl.when(to == me)
            def _():
                outward_own().start()

        return carry

    lax.fori_loop(0, count // per_tile, one_tile, 0)

    def finish(step, carry):
        to = lax.rem(me + step, count)
        outward(to).wait_send()
        pltpu.make_async_remote_copy(
            src_ref=mixed.at[rows(to), :],
            dst_ref=attend_out.at[:, columns(to)],
            send_sem=back_send.at[to],
            recv_sem=back_recv.at[to],
            device_id=(to, core),
            device_id_type=MESH,
        ).wait_recv()
        return carry

    lax.fori_loop(1, count, finish, 0)
    outward_own().wait()
    each_weight(lambda copy: copy.wait_send(), lambda copy: copy.wait())

    def weight_arrived(slot, carry):
        from_place, from_apart = slot // 2, lax.rem(slot, 2)
        sender = core * half + from_place
        mine = (sender == me) & (from_apart == 0)

        @pl.when(jnp.logical_not(mine))
        def _():
            for kind in range(2):
                left = pl.multiple_of((from_apart * 2 + kind) * HEAD_SIZE, HEAD_SIZE)
                view = weight_out.at[rows(from_place, depth), pl.ds(left, HEAD_SIZE)]
                pltpu.make_async_remote_copy(
                    src_ref=view,
                    dst_ref=view,
                    send_sem=w_send.at[kind, 0],
                    recv_sem=w_recv.at[kind, slot],
                    device_id=(me, 1 - core),
                    device_id_type=MESH,
                ).wait_recv()

        return carry

    lax.fori_loop(0, count, weight_arrived, 0)


def first_attention(count, band, queries, keys, values, low, wq, wk, wv):
    tok = queries.shape[0]
    tokens = tok * count
    whole = (tokens, HEAD_SIZE)
    dma = pltpu.SemaphoreType.DMA
    vmem = pl.BlockSpec(memory_space=pltpu.VMEM)
    anywhere = pl.BlockSpec(memory_space=pl.ANY)
    return pl.pallas_call(
        partial(first_kernel, count, band),
        out_shape=(
            jax.ShapeDtypeStruct(queries.shape, jnp.bfloat16),
            jax.ShapeDtypeStruct((wq.shape[0] * count // 2, 4 * HEAD_SIZE), jnp.bfloat16),
        ),
        in_specs=[vmem] * 4 + [anywhere] * 3,
        out_specs=(anywhere, anywhere),
        scratch_shapes=[pltpu.VMEM(whole, jnp.bfloat16)] * 4
        + [
            dma((3, count)),
            dma((3, count)),
            dma((3,)),
            dma((count,)),
            dma((count,)),
            dma,
            dma((2, count)),
            dma((2, count)),
            dma((2,)),
        ],
        compiler_params=pltpu.CompilerParams(
            collective_id=0, has_side_effects=True, vmem_limit_bytes=48 * 1024 * 1024
        ),
        name="first_attention",
    )(queries, keys, values, low, wq, wk, wv)


def second_kernel(
    count,
    band,
    normed_ref,
    weight_ref,
    cosine_ref,
    sine_ref,
    low_ref,
    attend_out,
    held,
    kept,
    away,
    arrived,
    query_all,
    pair_all,
    mixed,
    hop_send,
    hop_recv,
    core_send,
    core_recv,
    pair_send,
    pair_recv,
    back_send,
    back_recv,
    back_own,
):
    me, core = lax.axis_index("ctx"), lax.axis_index("heads")
    tok = normed_ref.shape[0]
    half = tok // 2
    deep = count // 4
    level = me // 4
    line_rows = deep * tok
    two_heads = 2 * HEAD_SIZE
    flip_one = me + 1 - 2 * lax.rem(me, 2)
    flip_two = me + 2 - 4 * lax.rem(me // 2, 2)
    flip_both = flip_one + flip_two - me
    near = (flip_two, flip_one)
    far = (flip_one, flip_two)
    greet_all(count)

    def place(owner):
        return (lax.rem(owner, 4) * deep + owner // 4) * tok

    def piece(part, owner):
        return held.at[pl.ds(pl.multiple_of(place(owner) + part * half, half), half), :]

    def hop(part, owner, way):
        to = (me + 4, me - 4, near[part], far[part])[way]
        return pltpu.make_async_remote_copy(
            src_ref=piece(part, owner),
            dst_ref=piece(part, owner),
            send_sem=hop_send.at[part, way, owner],
            recv_sem=hop_recv.at[part, owner],
            device_id=(to, core),
            device_id_type=MESH,
        )

    def came(part, owner):
        pltpu.make_async_remote_copy(
            src_ref=piece(part, owner),
            dst_ref=piece(part, owner),
            send_sem=hop_send.at[part, 0, owner],
            recv_sem=hop_recv.at[part, owner],
            device_id=(flip_one, core),
            device_id_type=MESH,
        ).wait_recv()

    def on_line(part, away_by, act, wait):
        for up in (True, False):
            owner = me - 4 * away_by if up else me + 4 * away_by
            there = level >= away_by if up else level + away_by < deep
            onward = level < deep - 1 if up else level > 0

            @pl.when(there)
            def _():
                if wait:
                    came(part, owner)

                @pl.when(onward)
                def _():
                    act(hop(part, owner, 0 if up else 1))

                if away_by > 0 or up:
                    act(hop(part, owner, 2))
                    act(hop(part, owner, 3))

    def on_next(part, away_by, act, wait):
        for up in (True, False):
            if away_by == 0 and not up:
                continue
            owner = near[part] - 4 * away_by if up else near[part] + 4 * away_by
            there = level >= away_by if up else level + away_by < deep

            @pl.when(there)
            def _():
                if wait:
                    came(part, owner)
                act(hop(part, owner, 3))

    def begin(copy):
        copy.start()

    held[pl.ds(pl.multiple_of(place(me), tok), tok), :] = normed_ref[...]
    for away_by in range(deep + 1):
        for part in range(2):
            if away_by < deep:
                on_line(part, away_by, begin, away_by > 0)
        for part in range(2):
            if away_by > 0:
                on_next(part, away_by - 1, begin, True)

    def core_copy(number):
        rows = pl.ds(number * line_rows, line_rows)
        return pltpu.make_async_remote_copy(
            src_ref=away.at[rows, :],
            dst_ref=arrived.at[rows, :],
            send_sem=core_send.at[number],
            recv_sem=core_recv.at[number],
            device_id=(me, 1 - core),
            device_id_type=MESH,
        )

    chunk = 256

    def multiply(number, lead):
        source = lax.rem(lead, 4) * line_rows

        def one(index, carry):
            block = held[pl.ds(pl.multiple_of(source + index * chunk, chunk), chunk), :]
            product = jnp.dot(block, weight_ref[...], preferred_element_type=jnp.float32)
            rows = pl.ds(pl.multiple_of(number * line_rows + index * chunk, chunk), chunk)
            kept[rows, :] = product[:, :two_heads]
            away[rows, :] = product[:, two_heads:]
            return carry

        lax.fori_loop(0, line_rows // chunk, one, 0)
        core_copy(number).start()

    which = lax.rem(me, 2)

    def token_rows(owner):
        return pl.ds(pl.multiple_of(owner * tok, tok), tok)

    def pair_copy(owner):
        return pltpu.make_async_remote_copy(
            src_ref=pair_all.at[which, token_rows(owner), :],
            dst_ref=pair_all.at[which, token_rows(owner), :],
            send_sem=pair_send.at[owner],
            recv_sem=pair_recv.at[owner],
            device_id=(flip_one, core),
            device_id_type=MESH,
        )

    def pair_came(owner):
        view = pair_all.at[1 - which, token_rows(owner), :]
        pltpu.make_async_remote_copy(
            src_ref=view,
            dst_ref=view,
            send_sem=pair_send.at[owner],
            recv_sem=pair_recv.at[owner],
            device_id=(flip_one, core),
            device_id_type=MESH,
        ).wait_recv()

    def settle(number, lead):
        core_copy(number).wait()

        def one(index, carry):
            owner = index * 4 + lax.rem(lead, 4)
            rows = pl.ds(pl.multiple_of(number * line_rows + index * tok, tok), tok)
            total = kept[rows, :] + arrived[rows, :]
            cosine = cosine_ref[token_rows(owner), :]
            sine = sine_ref[token_rows(owner), :]
            query = total[:, :HEAD_SIZE]
            other = total[:, HEAD_SIZE:]
            query_all[token_rows(owner), :] = (
                query * cosine + pltpu.roll(query, HEAD_SIZE // 2, 1) * sine
            ).astype(jnp.bfloat16)
            turned = other * cosine + pltpu.roll(other, HEAD_SIZE // 2, 1) * sine
            pair_all[which, token_rows(owner), :] = jnp.where(which == 0, turned, other).astype(
                jnp.bfloat16
            )
            pair_copy(owner).start()
            return carry

        lax.fori_loop(0, deep, one, 0)

    def line_came(part, lead):
        def one(index, carry):
            came(part, index * 4 + lax.rem(lead, 4))
            return carry

        lax.fori_loop(0, deep, one, 0)

    multiply(0, me)
    line_came(1, flip_two)
    multiply(1, flip_two)
    settle(0, me)
    line_came(0, flip_one)
    multiply(2, flip_one)
    settle(1, flip_two)
    settle(2, flip_one)
    line_came(0, flip_both)
    line_came(1, flip_both)
    multiply(3, flip_both)
    settle(3, flip_both)

    def pair_done(owner, carry):
        pair_copy(owner).wait_send()
        pair_came(owner)
        return carry

    lax.fori_loop(0, count, pair_done, 0)

    blocks = 2 * count
    own_columns = pl.ds(pl.multiple_of(me * HEAD_SIZE, HEAD_SIZE), HEAD_SIZE)

    def home(block):
        odd = lax.rem(block, 2)
        return jnp.where(odd == 0, block // 2, (blocks - 1 - block) // 2), odd

    def rows(index):
        return pl.ds(pl.multiple_of(index * half, half), half)

    def outward(block, to, odd):
        return pltpu.make_async_remote_copy(
            src_ref=mixed.at[rows(block), :],
            dst_ref=attend_out.at[rows(odd), own_columns],
            send_sem=back_send.at[block],
            recv_sem=back_recv.at[odd, me],
            device_id=(to, core),
            device_id_type=MESH,
        )

    def outward_own(block, odd):
        return pltpu.make_async_copy(
            mixed.at[rows(block), :], attend_out.at[rows(odd), own_columns], back_own.at[odd]
        )

    per_tile = QUERY_TILE // half

    def one_tile(tile, carry):
        attend_tile(
            tile, band, query_all, pair_all.at[0], pair_all.at[1], low_ref, mixed
        )
        for part in range(per_tile):
            block = tile * per_tile + part
            to, odd = home(block)

            @pl.when(to != me)
            def _():
                outward(block, to, odd).start()

            @pl.when(to == me)
            def _():
                outward_own(block, odd).start()

        return carry

    lax.fori_loop(0, blocks // per_tile, one_tile, 0)

    def sent(copy):
        copy.wait_send()

    for away_by in range(deep):
        for part in range(2):
            on_line(part, away_by, sent, False)
            on_next(part, away_by, sent, False)

    def finish(block, carry):
        to, odd = home(block)

        @pl.when(to != me)
        def _():
            outward(block, to, odd).wait_send()

        @pl.when(to == me)
        def _():
            outward_own(block, odd).wait()

        return carry

    lax.fori_loop(0, blocks, finish, 0)

    def landed(step, carry):
        sender = lax.rem(me + step, count)
        left = pl.multiple_of(sender * HEAD_SIZE, HEAD_SIZE)
        for odd in range(2):
            view = attend_out.at[pl.ds(odd * half, half), pl.ds(left, HEAD_SIZE)]
            pltpu.make_async_remote_copy(
                src_ref=view,
                dst_ref=view,
                send_sem=back_send.at[0],
                recv_sem=back_recv.at[odd, sender],
                device_id=(sender, core),
                device_id_type=MESH,
            ).wait_recv()
        return carry

    lax.fori_loop(1, count, landed, 0)


def second_layer(count, band, normed, weights, cosine, sine, low):
    tok, width = normed.shape
    tokens = tok * count
    dma = pltpu.SemaphoreType.DMA
    vmem = pl.BlockSpec(memory_space=pltpu.VMEM)
    wide = pltpu.VMEM((tokens, 2 * HEAD_SIZE), jnp.float32)
    return pl.pallas_call(
        partial(second_kernel, count, band),
        out_shape=jax.ShapeDtypeStruct((tok, count * HEAD_SIZE), jnp.bfloat16),
        in_specs=[vmem] * 5,
        out_specs=pl.BlockSpec(memory_space=pl.ANY),
        scratch_shapes=[
            pltpu.VMEM((tokens, width), jnp.bfloat16),
            wide,
            wide,
            wide,
            pltpu.VMEM((tokens, HEAD_SIZE), jnp.bfloat16),
            pltpu.VMEM((2, tokens, HEAD_SIZE), jnp.bfloat16),
            pltpu.VMEM((tokens, HEAD_SIZE), jnp.bfloat16),
            dma((2, 4, count)),
            dma((2, count)),
            dma((4,)),
            dma((4,)),
            dma((count,)),
            dma((count,)),
            dma((2 * count,)),
            dma((2, count)),
            dma((2,)),
        ],
        compiler_params=pltpu.CompilerParams(
            collective_id=1, has_side_effects=True, vmem_limit_bytes=56 * 1024 * 1024
        ),
        name="second_layer",
    )(normed, weights, cosine, sine, low)


def rotary_tables(positions):
    half_dim = HEAD_SIZE // 2
    speeds = THETA ** (-(jnp.arange(half_dim, dtype=jnp.float32) * 2.0 / HEAD_SIZE))
    angles = (positions.astype(jnp.float32) * POSITION_FACTOR)[:, None] * speeds[None, :]
    cosine, sine = jnp.cos(angles), jnp.sin(angles)
    return (
        jnp.concatenate([cosine, cosine], axis=1),
        jnp.concatenate([-sine, sine], axis=1),
    )


def to_other_core(block):
    return lax.ppermute(block, "heads", [(0, 1), (1, 0)])


def shards_by_head(
    count,
    resid_in,
    first_layer_queries,
    first_layer_keys,
    first_layer_values,
    out_one,
    post_gain,
    pre_gain,
    proj_query,
    key_projection,
    value_projection,
    window,
    positions,
):
    me, core = lax.axis_index("ctx"), lax.axis_index("heads")
    col_width = resid_in.shape[1]
    tokens = positions.shape[0]
    token = jnp.arange(tokens, dtype=jnp.int32)
    document = token - positions
    own_window = lax.dynamic_index_in_dim(window, me, 0, keepdims=False)
    low_one = jnp.maximum(document, token - own_window + 1)
    resid_other = to_other_core(resid_in)
    attend_one, weights = first_attention(
        count,
        LONGEST_WINDOW,
        first_layer_queries,
        first_layer_keys,
        first_layer_values,
        low_one[:, None],
        proj_query,
        key_projection,
        value_projection,
    )
    partial_rows = jnp.dot(attend_one, out_one, preferred_element_type=jnp.float32).astype(
        jnp.bfloat16
    )
    combined = partial_rows.astype(jnp.float32) + to_other_core(partial_rows).astype(jnp.float32)
    post_scaled = combined * lax.rsqrt(
        jnp.mean(combined * combined, axis=1, keepdims=True) + EPS
    )
    resid_row = jnp.where(
        core == 0,
        jnp.concatenate([resid_in, resid_other], axis=1),
        jnp.concatenate([resid_other, resid_in], axis=1),
    )
    resid_full = (resid_row.astype(jnp.float32) + post_gain[None, :] * post_scaled).astype(
        jnp.bfloat16
    )
    resid_out = lax.dynamic_slice_in_dim(resid_full, core * col_width, col_width, 1)
    widened = resid_full.astype(jnp.float32)
    factor = lax.rsqrt(jnp.mean(widened * widened, axis=1, keepdims=True) + EPS)
    gain_slice = lax.dynamic_slice_in_dim(pre_gain, core * col_width, col_width, 0)
    normed = (gain_slice[None, :] * resid_out.astype(jnp.float32) * factor).astype(jnp.bfloat16)
    cosine, sine = rotary_tables(positions)
    attended = second_layer(
        count, tokens // 2, normed, weights, cosine, sine, document[:, None]
    )
    return (resid_out, attended)


def solution(mesh):
    placed = (
        P("ctx", "heads"),
        P("ctx", "heads"),
        P("ctx", "heads"),
        P("ctx", "heads"),
        P("heads", None),
        P(),
        P(),
        P("ctx", "heads"),
        P("ctx", "heads"),
        P("ctx", "heads"),
        P("heads"),
        P(),
    )
    return jax.shard_map(
        partial(shards_by_head, mesh.shape["ctx"])
        if spread_fits(mesh)
        else shards,
        mesh=mesh,
        in_specs=placed,
        out_specs=(P("ctx", "heads"), P("ctx", "heads")),
        check_vma=False,
    )
```

```python
from functools import partial

import jax
import jax.numpy as jnp
from jax import lax
from jax.experimental import pallas as pl
from jax.experimental.pallas import tpu as pltpu
from jax.sharding import PartitionSpec as P

MODEL_WIDTH = 5376
HEAD_SIZE = 128
LONGEST_WINDOW = 1024


SCALE = 168.0 ** (-0.5)
EPS = 1e-06
THETA = 1000000.0
POSITION_FACTOR = 0.125


def shifted(value, axis, steps):
    count = lax.axis_size(axis)
    leading, last = (max(0, -steps), min(count, count - steps))
    return lax.ppermute(value, axis, [(source, source + steps) for source in range(leading, last)])


def from_partner(block, axis, bit):
    count = lax.axis_size(axis)
    route = []
    for low in range(count):
        high = low | 1 << bit
        if high != low and high < count:
            route += [(low, high), (high, low)]
    return lax.ppermute(block, axis, route)


def apply_rotary(values, pos_rows, factor):
    half_dim = values.shape[-1] // 2
    speeds = THETA ** (-(jnp.arange(half_dim, dtype=jnp.float32) * 2.0 / values.shape[-1]))
    angles = (pos_rows.astype(jnp.float32) * factor)[:, None] * speeds[None, :]
    cosine = jnp.cos(angles)[:, None, :]
    sine_part = jnp.sin(angles)[:, None, :]
    front_half = values[..., :half_dim]
    back_half = values[..., half_dim:]
    return jnp.concatenate(
        [front_half * cosine - back_half * sine_part, back_half * cosine + front_half * sine_part],
        axis=-1,
    )


def lookup(position_table, tokens):
    return jnp.take(position_table, jnp.clip(tokens, 0, position_table.shape[0] - 1))


def zig_token(row_ids, tok_dev):
    half_rows = tok_dev // 2
    device_of = row_ids // tok_dev
    local_row = row_ids % tok_dev
    last_pair = 2 * lax.axis_size("ctx") - 1
    return jnp.where(
        local_row < half_rows,
        2 * device_of * half_rows + local_row,
        (last_pair - 2 * device_of) * half_rows + local_row - half_rows,
    )


def masked_attention(
    query_row_block,
    key_row_block,
    value_row_block,
    query_tok,
    key_tok,
    query_pos,
    key_pos,
    window_limits,
):
    scores = (
        jnp.einsum(
            "qagd,kad->qagk", query_row_block, key_row_block, preferred_element_type=jnp.float32
        )
        * SCALE
    )
    distance = query_tok[:, None] - key_tok[None, :]
    base_ok = (
        (distance >= 0)
        & (key_tok[None, :] >= 0)
        & (query_pos[:, None] - key_pos[None, :] == distance)
    )
    visible = base_ok[:, None, None, :] & (
        distance[:, None, None, :] < window_limits[None, :, :, None]
    )
    row_peak = jnp.max(jnp.where(visible, scores, -1e30), axis=-1, keepdims=True)
    lifted = jnp.where(visible, jnp.exp(scores - row_peak), 0.0)
    row_total = jnp.sum(lifted, axis=-1)
    mixed = jnp.einsum(
        "qagk,kad->qagd",
        lifted.astype(jnp.bfloat16),
        value_row_block,
        preferred_element_type=jnp.float32,
    )
    return (mixed / row_total[..., None]).astype(jnp.bfloat16)


def mirror(rows_block, mover):
    half_rows = rows_block.shape[0] // 2
    travel = rows_block[half_rows:]
    bit_count = lax.axis_size("ctx").bit_length() - 1
    for bit_index in range(bit_count):
        travel = mover(travel, bit_index)
    return jnp.concatenate([rows_block[:half_rows], travel], axis=0)


def project(residual_rows, pre_gain, proj_query, key_projection, value_projection, row_pos):
    row_count = residual_rows.shape[0]
    widened = residual_rows.astype(jnp.float32)
    normalized_rows = (
        pre_gain[None, :]
        * widened
        * lax.rsqrt(jnp.mean(widened * widened, axis=1, keepdims=True) + EPS)
    ).astype(jnp.bfloat16)
    query_heads = proj_query.shape[1] // HEAD_SIZE
    pair_heads = key_projection.shape[1] // HEAD_SIZE
    second_layer_query = (
        apply_rotary(
            jnp.dot(
                normalized_rows,
                lax.all_gather(proj_query, "ctx", axis=0, tiled=True),
                preferred_element_type=jnp.float32,
            ).reshape(row_count, query_heads, HEAD_SIZE),
            row_pos,
            POSITION_FACTOR,
        )
        .astype(jnp.bfloat16)
        .reshape(row_count, query_heads * HEAD_SIZE)
    )
    second_layer_key = (
        apply_rotary(
            jnp.dot(
                normalized_rows,
                lax.all_gather(key_projection, "ctx", axis=0, tiled=True),
                preferred_element_type=jnp.float32,
            ).reshape(row_count, pair_heads, HEAD_SIZE),
            row_pos,
            POSITION_FACTOR,
        )
        .astype(jnp.bfloat16)
        .reshape(row_count, pair_heads * HEAD_SIZE)
    )
    second_layer_value = jnp.dot(
        normalized_rows,
        lax.all_gather(value_projection, "ctx", axis=0, tiled=True),
        preferred_element_type=jnp.float32,
    ).astype(jnp.bfloat16)
    return (second_layer_query, second_layer_key, second_layer_value)


def attend_block(
    state, query_row_block, key_block, value_block, query_tok, query_pos, block_tok, block_pos
):
    row_peak, row_total, weighted = state
    scores = (
        jnp.einsum("qagd,kad->qagk", query_row_block, key_block, preferred_element_type=jnp.float32)
        * SCALE
    )
    distance = query_tok[:, None] - block_tok[None, :]
    visible = (distance >= 0) & (query_pos[:, None] - block_pos[None, :] == distance)
    visible = visible[:, None, None, :]
    new_peak = jnp.maximum(row_peak, jnp.max(jnp.where(visible, scores, -1e30), axis=-1))
    lifted = jnp.where(visible, jnp.exp(scores - new_peak[..., None]), 0.0)
    shrink = jnp.exp(row_peak - new_peak)
    row_total = row_total * shrink + jnp.sum(lifted, axis=-1)
    weighted = weighted * shrink[..., None] + jnp.einsum(
        "qagk,kad->qagd",
        lifted.astype(jnp.bfloat16),
        value_block,
        preferred_element_type=jnp.float32,
    )
    return (new_peak, row_total, weighted)


def keep_state(state):
    return state


def shards(
    resid_in,
    first_layer_queries,
    first_layer_keys,
    first_layer_values,
    out_one,
    post_gain,
    pre_gain,
    proj_query,
    key_projection,
    value_projection,
    window,
    positions,
):
    tok_dev = resid_in.shape[0]
    col_width = resid_in.shape[1]
    ctx_place = lax.axis_index("ctx")
    head_place = lax.axis_index("heads")
    query_heads = first_layer_queries.shape[1] // HEAD_SIZE
    pair_heads = first_layer_keys.shape[1] // HEAD_SIZE
    group_length = query_heads // pair_heads
    window_limits = window.reshape(pair_heads, group_length)
    own_pairs = jnp.stack([first_layer_keys, first_layer_values])
    reach_count = LONGEST_WINDOW // tok_dev
    pieces = [own_pairs]
    for section in range(reach_count):
        pieces = [shifted(own_pairs, "ctx", section + 1)] + pieces
    extended = jnp.concatenate(pieces, axis=1)
    key_span = extended.shape[1]
    local_tok = ctx_place * tok_dev + jnp.arange(tok_dev, dtype=jnp.int32)
    key_tok = (ctx_place - reach_count) * tok_dev + jnp.arange(key_span, dtype=jnp.int32)
    attend_one = masked_attention(
        first_layer_queries.reshape(tok_dev, pair_heads, group_length, HEAD_SIZE),
        extended[0].reshape(key_span, pair_heads, HEAD_SIZE),
        extended[1].reshape(key_span, pair_heads, HEAD_SIZE),
        local_tok,
        key_tok,
        lookup(positions, local_tok),
        lookup(positions, key_tok),
        window_limits,
    )
    attend_one = attend_one.reshape(tok_dev, query_heads * HEAD_SIZE)
    partial_rows = jnp.dot(attend_one, out_one, preferred_element_type=jnp.float32)
    mirror_tok = zig_token(ctx_place * tok_dev + jnp.arange(tok_dev, dtype=jnp.int32), tok_dev)
    mirror_pos = lookup(positions, mirror_tok)
    shared = lax.psum_scatter(
        partial_rows.astype(jnp.bfloat16), "heads", scatter_dimension=1, tiled=True
    ).astype(jnp.float32)
    squares = lax.psum(jnp.sum(shared * shared, axis=1), "heads")
    post_scaled = shared * lax.rsqrt(squares[:, None] / MODEL_WIDTH + EPS)
    gain_slice = lax.dynamic_slice_in_dim(post_gain, head_place * col_width, col_width, 0)
    resid_out = (resid_in.astype(jnp.float32) + gain_slice[None, :] * post_scaled).astype(
        jnp.bfloat16
    )

    def move_resid(piece, bit_index):
        return from_partner(piece, "ctx", bit_index)

    relayed = mirror(resid_out, move_resid)
    residual_rows = lax.all_gather(relayed, "heads", axis=1, tiled=True)
    second_layer_query, second_layer_key, second_layer_value = project(
        residual_rows, pre_gain, proj_query, key_projection, value_projection, mirror_pos
    )
    half_rows = tok_dev // 2
    queries = second_layer_query.reshape(tok_dev, pair_heads, group_length, HEAD_SIZE)
    query_parts = (queries[:half_rows], queries[half_rows:])
    tok_parts = (mirror_tok[:half_rows], mirror_tok[half_rows:])
    pos_parts = (mirror_pos[:half_rows], mirror_pos[half_rows:])
    pair_two = jnp.stack([second_layer_key, second_layer_value])

    def empty_state():
        return (
            jnp.full((half_rows, pair_heads, group_length), -1e30, jnp.float32),
            jnp.zeros((half_rows, pair_heads, group_length), jnp.float32),
            jnp.zeros((half_rows, pair_heads, group_length, HEAD_SIZE), jnp.float32),
        )

    start_state = (empty_state(), empty_state())
    piece = lax.all_gather(pair_two, "ctx", axis=1, tiled=True)
    piece_rows = piece.shape[1]
    unit_rows = 2 * tok_dev
    unit_count = piece_rows // unit_rows

    def one_unit(index, state):
        offset = index * unit_rows
        unit_block = lax.dynamic_slice_in_dim(piece, offset, unit_rows, 1)
        current = list(state)
        for key_half in range(unit_rows // half_rows):
            key_block = unit_block[0, key_half * half_rows : (key_half + 1) * half_rows].reshape(
                half_rows, pair_heads, HEAD_SIZE
            )
            value_block = unit_block[1, key_half * half_rows : (key_half + 1) * half_rows].reshape(
                half_rows, pair_heads, HEAD_SIZE
            )
            key_row_block = offset + key_half * half_rows + jnp.arange(half_rows, dtype=jnp.int32)
            block_tok = zig_token(key_row_block, tok_dev)
            block_pos = lookup(positions, block_tok)
            earliest = jnp.min(block_tok)
            for query_half in range(2):
                work = partial(
                    attend_block,
                    query_row_block=query_parts[query_half],
                    key_block=key_block,
                    value_block=value_block,
                    query_tok=tok_parts[query_half],
                    query_pos=pos_parts[query_half],
                    block_tok=block_tok,
                    block_pos=block_pos,
                )
                needed = earliest <= tok_parts[query_half][half_rows - 1]
                current[query_half] = lax.cond(needed, work, keep_state, current[query_half])
        return tuple(current)

    final_state = lax.fori_loop(0, unit_count, one_unit, start_state)
    front = final_state[0][2] / final_state[0][1][..., None]
    back = final_state[1][2] / final_state[1][1][..., None]
    attended = (
        jnp.concatenate([front, back], axis=0)
        .astype(jnp.bfloat16)
        .reshape(tok_dev, query_heads * HEAD_SIZE)
    )
    return (resid_out, attended)


MESH = pl.DeviceIdType.MESH
QUERY_TILE = 256


def early_rows(depth):
    return depth * 2 // 7 // 16 * 16


def spread_fits(mesh):
    return mesh.shape["heads"] == 2 and mesh.shape["ctx"] == 16


def greet_all(count):
    me, core = lax.axis_index("ctx"), lax.axis_index("heads")
    barrier = pltpu.get_barrier_semaphore()

    def greet(step, carry):
        pl.semaphore_signal(
            barrier, inc=1, device_id=(lax.rem(me + step, count), core), device_id_type=MESH
        )
        pl.semaphore_signal(
            barrier, inc=1, device_id=(lax.rem(me + step, count), 1 - core), device_id_type=MESH
        )
        return carry

    lax.fori_loop(1, count, greet, 0)
    pl.semaphore_signal(barrier, inc=1, device_id=(me, 1 - core), device_id_type=MESH)
    pl.semaphore_wait(barrier, 2 * count - 1)


def attend_tile(tile, band, query_ref, key_ref, value_ref, low_ref, mixed_ref):
    tokens = query_ref.shape[0]
    span = min(band + QUERY_TILE, tokens)
    first = pl.multiple_of(tile * QUERY_TILE, QUERY_TILE)
    begin = pl.multiple_of(jnp.maximum(first + QUERY_TILE - span, 0), QUERY_TILE)
    scores = (
        lax.dot_general(
            query_ref[pl.ds(first, QUERY_TILE), :],
            key_ref[pl.ds(begin, span), :],
            (((1,), (1,)), ((), ())),
            preferred_element_type=jnp.float32,
        )
        * SCALE
    )
    rows = first + lax.broadcasted_iota(jnp.int32, (QUERY_TILE, 1), 0)
    columns = begin + lax.broadcasted_iota(jnp.int32, (1, span), 1)
    visible = (columns <= rows) & (columns >= low_ref[pl.ds(first, QUERY_TILE), :])
    scores = jnp.where(visible, scores, -1e30)
    lifted = jnp.exp(scores - jnp.max(scores, axis=1, keepdims=True))
    total = jnp.sum(lifted, axis=1, keepdims=True)
    mixed = jnp.dot(
        lifted.astype(jnp.bfloat16),
        value_ref[pl.ds(begin, span), :],
        preferred_element_type=jnp.float32,
    )
    mixed_ref[pl.ds(first, QUERY_TILE), :] = (mixed / total).astype(jnp.bfloat16)


def weight_spread(count, sources, target, first, size, stride, offset, w_send, w_recv, w_own):
    me, core = lax.axis_index("ctx"), lax.axis_index("heads")
    half = count // 2
    to_core = me // half
    place = lax.rem(me, half)
    apart = jnp.where(to_core == core, 0, 1)
    wq_ref, wk_ref, wv_ref = sources

    def spot(from_place, slot):
        top = pl.multiple_of(from_place * stride + offset, 16)
        left = pl.multiple_of(slot * HEAD_SIZE, HEAD_SIZE)
        return target.at[pl.ds(top, size), pl.ds(left, HEAD_SIZE)]

    def block(ref, index):
        left = pl.multiple_of(index * HEAD_SIZE, HEAD_SIZE)
        return ref.at[pl.ds(first, size), pl.ds(left, HEAD_SIZE)]

    def views(pair, odd):
        second = wk_ref if odd == 0 else wv_ref
        return (
            (block(wq_ref, 2 * pair + odd), spot(place, apart * 2)),
            (block(second, pair), spot(place, apart * 2 + 1)),
        )

    def remote(pair, odd):
        to = 2 * pair + odd
        return [
            pltpu.make_async_remote_copy(
                src_ref=source,
                dst_ref=landing,
                send_sem=w_send.at[kind, to],
                recv_sem=w_recv.at[kind, place * 2 + apart],
                device_id=(to, to_core),
                device_id_type=MESH,
            )
            for kind, (source, landing) in enumerate(views(pair, odd))
        ]

    def local(pair, odd):
        return [
            pltpu.make_async_copy(source, landing, w_own.at[kind])
            for kind, (source, landing) in enumerate(views(pair, odd))
        ]

    def each(low, high, act_remote, act_local):
        def body(pair, carry):
            for odd in range(2):
                mine = (2 * pair + odd == me) & (to_core == core)

                @pl.when(jnp.logical_not(mine))
                def _():
                    for copy in remote(pair, odd):
                        act_remote(copy)

                @pl.when(mine)
                def _():
                    for copy in local(pair, odd):
                        act_local(copy)

            return carry

        lax.fori_loop(low, high, body, 0)

    def one_arrived(slot, carry):
        from_place, from_apart = slot // 2, lax.rem(slot, 2)
        mine = (core * half + from_place == me) & (from_apart == 0)

        @pl.when(jnp.logical_not(mine))
        def _():
            for kind in range(2):
                view = spot(from_place, from_apart * 2 + kind)
                pltpu.make_async_remote_copy(
                    src_ref=view,
                    dst_ref=view,
                    send_sem=w_send.at[kind, 0],
                    recv_sem=w_recv.at[kind, slot],
                    device_id=(me, 1 - core),
                    device_id_type=MESH,
                ).wait_recv()

        return carry

    def start(low, high):
        each(low, high, lambda copy: copy.start(), lambda copy: copy.start())

    def finish():
        each(0, half, lambda copy: copy.wait_send(), lambda copy: copy.wait())
        lax.fori_loop(0, count, one_arrived, 0)

    return start, finish


def first_kernel(
    count,
    band,
    query_in,
    key_in,
    value_in,
    low_ref,
    wq_ref,
    wk_ref,
    wv_ref,
    attend_out,
    weight_out,
    query_all,
    key_all,
    value_all,
    mixed,
    in_send,
    in_recv,
    in_own,
    back_send,
    back_recv,
    back_own,
    w_send,
    w_recv,
    w_own,
):
    me, core = lax.axis_index("ctx"), lax.axis_index("heads")
    tok = query_in.shape[0]
    half = count // 2
    early = weight_out.shape[0] // half
    greet_all(count)

    def columns(index):
        return pl.ds(pl.multiple_of(index * HEAD_SIZE, HEAD_SIZE), HEAD_SIZE)

    def rows(index, size=tok):
        return pl.ds(pl.multiple_of(index * size, size), size)

    def inward(step):
        to = lax.rem(me + step, count)
        trio = (
            (query_in, query_all, to),
            (key_in, key_all, to // 2),
            (value_in, value_all, to // 2),
        )
        return [
            pltpu.make_async_remote_copy(
                src_ref=source.at[:, columns(block)],
                dst_ref=target.at[rows(me), :],
                send_sem=in_send.at[kind, step],
                recv_sem=in_recv.at[kind, step],
                device_id=(to, core),
                device_id_type=MESH,
            )
            for kind, (source, target, block) in enumerate(trio)
        ]

    def start_inward(step, carry):
        for copy in inward(step):
            copy.start()
        return carry

    def wait_inward(step, carry):
        for copy in inward(step):
            copy.wait()
        return carry

    lax.fori_loop(1, count, start_inward, 0)
    own = [
        pltpu.make_async_copy(source.at[:, columns(block)], target.at[rows(me), :], in_own.at[kind])
        for kind, (source, target, block) in enumerate(
            (
                (query_in, query_all, me),
                (key_in, key_all, me // 2),
                (value_in, value_all, me // 2),
            )
        )
    ]
    for copy in own:
        copy.start()
    for copy in own:
        copy.wait()
    lax.fori_loop(1, count, wait_inward, 0)

    weight_start, weight_finish = weight_spread(
        count, (wq_ref, wk_ref, wv_ref), weight_out, 0, early, early, 0, w_send, w_recv, w_own
    )
    weight_start(0, half)

    def outward(to):
        return pltpu.make_async_remote_copy(
            src_ref=mixed.at[rows(to), :],
            dst_ref=attend_out.at[:, columns(me)],
            send_sem=back_send.at[to],
            recv_sem=back_recv.at[me],
            device_id=(to, core),
            device_id_type=MESH,
        )

    def outward_own():
        return pltpu.make_async_copy(
            mixed.at[rows(me), :], attend_out.at[:, columns(me)], back_own
        )

    per_tile = QUERY_TILE // tok

    def one_tile(tile, carry):
        attend_tile(tile, band, query_all, key_all, value_all, low_ref, mixed)
        for part in range(per_tile):
            to = tile * per_tile + part

            @pl.when(to != me)
            def _():
                outward(to).start()

            @pl.when(to == me)
            def _():
                outward_own().start()

        return carry

    lax.fori_loop(0, count // per_tile, one_tile, 0)

    def finish(step, carry):
        to = lax.rem(me + step, count)
        outward(to).wait_send()
        pltpu.make_async_remote_copy(
            src_ref=mixed.at[rows(to), :],
            dst_ref=attend_out.at[:, columns(to)],
            send_sem=back_send.at[to],
            recv_sem=back_recv.at[to],
            device_id=(to, core),
            device_id_type=MESH,
        ).wait_recv()
        return carry

    lax.fori_loop(1, count, finish, 0)
    outward_own().wait()
    weight_finish()


def first_attention(count, band, early, queries, keys, values, low, wq, wk, wv):
    tok = queries.shape[0]
    tokens = tok * count
    whole = (tokens, HEAD_SIZE)
    dma = pltpu.SemaphoreType.DMA
    vmem = pl.BlockSpec(memory_space=pltpu.VMEM)
    anywhere = pl.BlockSpec(memory_space=pl.ANY)
    return pl.pallas_call(
        partial(first_kernel, count, band),
        out_shape=(
            jax.ShapeDtypeStruct(queries.shape, jnp.bfloat16),
            jax.ShapeDtypeStruct((early * count // 2, 4 * HEAD_SIZE), jnp.bfloat16),
        ),
        in_specs=[anywhere] * 3 + [vmem] + [anywhere] * 3,
        out_specs=(anywhere, anywhere),
        scratch_shapes=[pltpu.VMEM(whole, jnp.bfloat16)] * 4
        + [
            dma((3, count)),
            dma((3, count)),
            dma((3,)),
            dma((count,)),
            dma((count,)),
            dma,
            dma((2, count)),
            dma((2, count)),
            dma((2,)),
        ],
        compiler_params=pltpu.CompilerParams(
            collective_id=0, has_side_effects=True, vmem_limit_bytes=48 * 1024 * 1024
        ),
        name="first_attention",
    )(queries, keys, values, low, wq, wk, wv)


def second_kernel(
    count,
    band,
    normed_ref,
    early_ref,
    wq_ref,
    wk_ref,
    wv_ref,
    cosine_ref,
    sine_ref,
    low_ref,
    attend_out,
    weight_ref,
    held,
    kept,
    away,
    arrived,
    query_all,
    pair_all,
    mixed,
    hop_send,
    hop_recv,
    core_send,
    core_recv,
    pair_send,
    pair_recv,
    back_send,
    back_recv,
    back_own,
    w_send,
    w_recv,
    w_own,
    early_sem,
):
    me, core = lax.axis_index("ctx"), lax.axis_index("heads")
    tok = normed_ref.shape[0]
    half = tok // 2
    deep = count // 4
    level = me // 4
    line_rows = deep * tok
    two_heads = 2 * HEAD_SIZE
    flip_one = me + 1 - 2 * lax.rem(me, 2)
    flip_two = me + 2 - 4 * lax.rem(me // 2, 2)
    flip_both = flip_one + flip_two - me
    near = (flip_two, flip_one)
    far = (flip_one, flip_two)
    greet_all(count)

    def place(owner):
        return (lax.rem(owner, 4) * deep + owner // 4) * tok

    def piece(part, owner):
        return held.at[pl.ds(pl.multiple_of(place(owner) + part * half, half), half), :]

    def hop(part, owner, way):
        to = (me + 4, me - 4, near[part], far[part])[way]
        return pltpu.make_async_remote_copy(
            src_ref=piece(part, owner),
            dst_ref=piece(part, owner),
            send_sem=hop_send.at[part, way, owner],
            recv_sem=hop_recv.at[part, owner],
            device_id=(to, core),
            device_id_type=MESH,
        )

    def came(part, owner):
        pltpu.make_async_remote_copy(
            src_ref=piece(part, owner),
            dst_ref=piece(part, owner),
            send_sem=hop_send.at[part, 0, owner],
            recv_sem=hop_recv.at[part, owner],
            device_id=(flip_one, core),
            device_id_type=MESH,
        ).wait_recv()

    def on_line(part, away_by, act, wait):
        for up in (True, False):
            owner = me - 4 * away_by if up else me + 4 * away_by
            there = level >= away_by if up else level + away_by < deep
            onward = level < deep - 1 if up else level > 0

            @pl.when(there)
            def _():
                if wait:
                    came(part, owner)

                @pl.when(onward)
                def _():
                    act(hop(part, owner, 0 if up else 1))

                if away_by > 0 or up:
                    act(hop(part, owner, 2))
                    act(hop(part, owner, 3))

    def on_next(part, away_by, act, wait):
        for up in (True, False):
            if away_by == 0 and not up:
                continue
            owner = near[part] - 4 * away_by if up else near[part] + 4 * away_by
            there = level >= away_by if up else level + away_by < deep

            @pl.when(there)
            def _():
                if wait:
                    came(part, owner)
                act(hop(part, owner, 3))

    def begin(copy):
        copy.start()

    held[pl.ds(pl.multiple_of(place(me), tok), tok), :] = normed_ref[...]
    depth = wq_ref.shape[0]
    places = count // 2
    early = early_ref.shape[0] // places
    weight_start, weight_finish = weight_spread(
        count,
        (wq_ref, wk_ref, wv_ref),
        weight_ref,
        early,
        depth - early,
        depth,
        early,
        w_send,
        w_recv,
        w_own,
    )
    batch = places // deep
    moved = [
        pltpu.make_async_copy(
            early_ref.at[pl.ds(index * early, early), :],
            weight_ref.at[pl.ds(index * depth, early), :],
            early_sem.at[index],
        )
        for index in range(places)
    ]
    for away_by in range(deep + 1):
        for part in range(2):
            if away_by < deep:
                on_line(part, away_by, begin, away_by > 0)
        for part in range(2):
            if away_by > 0:
                on_next(part, away_by - 1, begin, True)
        if away_by < deep:
            weight_start(away_by * batch, (away_by + 1) * batch)
        if away_by == 0:
            for copy in moved:
                copy.start()

    def core_copy(number):
        rows = pl.ds(number * line_rows, line_rows)
        return pltpu.make_async_remote_copy(
            src_ref=away.at[rows, :],
            dst_ref=arrived.at[rows, :],
            send_sem=core_send.at[number],
            recv_sem=core_recv.at[number],
            device_id=(me, 1 - core),
            device_id_type=MESH,
        )

    chunk = 256

    def multiply(number, lead):
        source = lax.rem(lead, 4) * line_rows

        def one(index, carry):
            block = held[pl.ds(pl.multiple_of(source + index * chunk, chunk), chunk), :]
            product = jnp.dot(block, weight_ref[...], preferred_element_type=jnp.float32)
            rows = pl.ds(pl.multiple_of(number * line_rows + index * chunk, chunk), chunk)
            kept[rows, :] = product[:, :two_heads]
            away[rows, :] = product[:, two_heads:]
            return carry

        lax.fori_loop(0, line_rows // chunk, one, 0)
        core_copy(number).start()

    which = lax.rem(me, 2)

    def token_rows(owner):
        return pl.ds(pl.multiple_of(owner * tok, tok), tok)

    def pair_copy(owner):
        return pltpu.make_async_remote_copy(
            src_ref=pair_all.at[which, token_rows(owner), :],
            dst_ref=pair_all.at[which, token_rows(owner), :],
            send_sem=pair_send.at[owner],
            recv_sem=pair_recv.at[owner],
            device_id=(flip_one, core),
            device_id_type=MESH,
        )

    def pair_came(owner):
        view = pair_all.at[1 - which, token_rows(owner), :]
        pltpu.make_async_remote_copy(
            src_ref=view,
            dst_ref=view,
            send_sem=pair_send.at[owner],
            recv_sem=pair_recv.at[owner],
            device_id=(flip_one, core),
            device_id_type=MESH,
        ).wait_recv()

    def settle(number, lead):
        core_copy(number).wait()

        def one(index, carry):
            owner = index * 4 + lax.rem(lead, 4)
            rows = pl.ds(pl.multiple_of(number * line_rows + index * tok, tok), tok)
            total = kept[rows, :] + arrived[rows, :]
            cosine = cosine_ref[token_rows(owner), :]
            sine = sine_ref[token_rows(owner), :]
            query = total[:, :HEAD_SIZE]
            other = total[:, HEAD_SIZE:]
            query_all[token_rows(owner), :] = (
                query * cosine + pltpu.roll(query, HEAD_SIZE // 2, 1) * sine
            ).astype(jnp.bfloat16)
            turned = other * cosine + pltpu.roll(other, HEAD_SIZE // 2, 1) * sine
            pair_all[which, token_rows(owner), :] = jnp.where(which == 0, turned, other).astype(
                jnp.bfloat16
            )
            pair_copy(owner).start()
            return carry

        lax.fori_loop(0, deep, one, 0)

    def line_came(part, lead):
        def one(index, carry):
            came(part, index * 4 + lax.rem(lead, 4))
            return carry

        lax.fori_loop(0, deep, one, 0)

    for copy in moved:
        copy.wait()
    weight_finish()
    multiply(0, me)
    line_came(1, flip_two)
    multiply(1, flip_two)
    settle(0, me)
    line_came(0, flip_one)
    multiply(2, flip_one)
    settle(1, flip_two)
    settle(2, flip_one)
    line_came(0, flip_both)
    line_came(1, flip_both)
    multiply(3, flip_both)
    settle(3, flip_both)

    def pair_done(owner, carry):
        pair_copy(owner).wait_send()
        pair_came(owner)
        return carry

    lax.fori_loop(0, count, pair_done, 0)

    blocks = 2 * count
    own_columns = pl.ds(pl.multiple_of(me * HEAD_SIZE, HEAD_SIZE), HEAD_SIZE)

    def home(block):
        odd = lax.rem(block, 2)
        return jnp.where(odd == 0, block // 2, (blocks - 1 - block) // 2), odd

    def rows(index):
        return pl.ds(pl.multiple_of(index * half, half), half)

    def outward(block, to, odd):
        return pltpu.make_async_remote_copy(
            src_ref=mixed.at[rows(block), :],
            dst_ref=attend_out.at[rows(odd), own_columns],
            send_sem=back_send.at[block],
            recv_sem=back_recv.at[odd, me],
            device_id=(to, core),
            device_id_type=MESH,
        )

    def outward_own(block, odd):
        return pltpu.make_async_copy(
            mixed.at[rows(block), :], attend_out.at[rows(odd), own_columns], back_own.at[odd]
        )

    per_tile = QUERY_TILE // half

    def one_tile(tile, carry):
        attend_tile(
            tile, band, query_all, pair_all.at[0], pair_all.at[1], low_ref, mixed
        )
        for part in range(per_tile):
            block = tile * per_tile + part
            to, odd = home(block)

            @pl.when(to != me)
            def _():
                outward(block, to, odd).start()

            @pl.when(to == me)
            def _():
                outward_own(block, odd).start()

        return carry

    lax.fori_loop(0, blocks // per_tile, one_tile, 0)

    def sent(copy):
        copy.wait_send()

    for away_by in range(deep):
        for part in range(2):
            on_line(part, away_by, sent, False)
            on_next(part, away_by, sent, False)

    def finish(block, carry):
        to, odd = home(block)

        @pl.when(to != me)
        def _():
            outward(block, to, odd).wait_send()

        @pl.when(to == me)
        def _():
            outward_own(block, odd).wait()

        return carry

    lax.fori_loop(0, blocks, finish, 0)

    def landed(step, carry):
        sender = lax.rem(me + step, count)
        left = pl.multiple_of(sender * HEAD_SIZE, HEAD_SIZE)
        for odd in range(2):
            view = attend_out.at[pl.ds(odd * half, half), pl.ds(left, HEAD_SIZE)]
            pltpu.make_async_remote_copy(
                src_ref=view,
                dst_ref=view,
                send_sem=back_send.at[0],
                recv_sem=back_recv.at[odd, sender],
                device_id=(sender, core),
                device_id_type=MESH,
            ).wait_recv()
        return carry

    lax.fori_loop(1, count, landed, 0)


def second_layer(count, band, normed, weights, wq, wk, wv, cosine, sine, low):
    tok, width = normed.shape
    tokens = tok * count
    dma = pltpu.SemaphoreType.DMA
    vmem = pl.BlockSpec(memory_space=pltpu.VMEM)
    anywhere = pl.BlockSpec(memory_space=pl.ANY)
    wide = pltpu.VMEM((tokens, 2 * HEAD_SIZE), jnp.float32)
    return pl.pallas_call(
        partial(second_kernel, count, band),
        out_shape=jax.ShapeDtypeStruct((tok, count * HEAD_SIZE), jnp.bfloat16),
        in_specs=[vmem] + [anywhere] * 4 + [vmem] * 3,
        out_specs=anywhere,
        scratch_shapes=[
            pltpu.VMEM((wq.shape[0] * count // 2, 4 * HEAD_SIZE), jnp.bfloat16),
            pltpu.VMEM((tokens, width), jnp.bfloat16),
            wide,
            wide,
            wide,
            pltpu.VMEM((tokens, HEAD_SIZE), jnp.bfloat16),
            pltpu.VMEM((2, tokens, HEAD_SIZE), jnp.bfloat16),
            pltpu.VMEM((tokens, HEAD_SIZE), jnp.bfloat16),
            dma((2, 4, count)),
            dma((2, count)),
            dma((4,)),
            dma((4,)),
            dma((count,)),
            dma((count,)),
            dma((2 * count,)),
            dma((2, count)),
            dma((2,)),
            dma((2, count)),
            dma((2, count)),
            dma((2,)),
            dma((count // 2,)),
        ],
        compiler_params=pltpu.CompilerParams(
            collective_id=1, has_side_effects=True, vmem_limit_bytes=56 * 1024 * 1024
        ),
        name="second_layer",
    )(normed, weights, wq, wk, wv, cosine, sine, low)


def rotary_tables(positions):
    half_dim = HEAD_SIZE // 2
    speeds = THETA ** (-(jnp.arange(half_dim, dtype=jnp.float32) * 2.0 / HEAD_SIZE))
    angles = (positions.astype(jnp.float32) * POSITION_FACTOR)[:, None] * speeds[None, :]
    cosine, sine = jnp.cos(angles), jnp.sin(angles)
    return (
        jnp.concatenate([cosine, cosine], axis=1),
        jnp.concatenate([-sine, sine], axis=1),
    )


def to_other_core(block):
    return lax.ppermute(block, "heads", [(0, 1), (1, 0)])


def shards_by_head(
    count,
    resid_in,
    first_layer_queries,
    first_layer_keys,
    first_layer_values,
    out_one,
    post_gain,
    pre_gain,
    proj_query,
    key_projection,
    value_projection,
    window,
    positions,
):
    me, core = lax.axis_index("ctx"), lax.axis_index("heads")
    col_width = resid_in.shape[1]
    tokens = positions.shape[0]
    token = jnp.arange(tokens, dtype=jnp.int32)
    document = token - positions
    own_window = lax.dynamic_index_in_dim(window, me, 0, keepdims=False)
    low_one = jnp.maximum(document, token - own_window + 1)
    resid_other = to_other_core(resid_in)
    early = early_rows(proj_query.shape[0])
    attend_one, weights = first_attention(
        count,
        LONGEST_WINDOW,
        early,
        first_layer_queries,
        first_layer_keys,
        first_layer_values,
        low_one[:, None],
        proj_query,
        key_projection,
        value_projection,
    )
    partial_rows = jnp.dot(attend_one, out_one, preferred_element_type=jnp.float32).astype(
        jnp.bfloat16
    )
    combined = partial_rows.astype(jnp.float32) + to_other_core(partial_rows).astype(jnp.float32)
    post_scaled = combined * lax.rsqrt(
        jnp.mean(combined * combined, axis=1, keepdims=True) + EPS
    )
    resid_row = jnp.where(
        core == 0,
        jnp.concatenate([resid_in, resid_other], axis=1),
        jnp.concatenate([resid_other, resid_in], axis=1),
    )
    resid_full = (resid_row.astype(jnp.float32) + post_gain[None, :] * post_scaled).astype(
        jnp.bfloat16
    )
    resid_out = lax.dynamic_slice_in_dim(resid_full, core * col_width, col_width, 1)
    widened = resid_full.astype(jnp.float32)
    factor = lax.rsqrt(jnp.mean(widened * widened, axis=1, keepdims=True) + EPS)
    gain_slice = lax.dynamic_slice_in_dim(pre_gain, core * col_width, col_width, 0)
    normed = (gain_slice[None, :] * resid_out.astype(jnp.float32) * factor).astype(jnp.bfloat16)
    cosine, sine = rotary_tables(positions)
    attended = second_layer(
        count,
        tokens // 2,
        normed,
        weights,
        proj_query,
        key_projection,
        value_projection,
        cosine,
        sine,
        document[:, None],
    )
    return (resid_out, attended)


def solution(mesh):
    placed = (
        P("ctx", "heads"),
        P("ctx", "heads"),
        P("ctx", "heads"),
        P("ctx", "heads"),
        P("heads", None),
        P(),
        P(),
        P("ctx", "heads"),
        P("ctx", "heads"),
        P("ctx", "heads"),
        P("heads"),
        P(),
    )
    return jax.shard_map(
        partial(shards_by_head, mesh.shape["ctx"])
        if spread_fits(mesh)
        else shards,
        mesh=mesh,
        in_specs=placed,
        out_specs=(P("ctx", "heads"), P("ctx", "heads")),
        check_vma=False,
    )
```
